256 devices in a mesh: sec: 16 (over x, y), grp: 16 (over z, core).
Axes of the slice: x: 4, y: 4, z: 8, core: 2. Of those that a mesh axis runs over, the one named last changes fastest.
Arguments:
- queries: bfloat16 [32768, 2048], P(('sec', 'grp')), may hold values from -6 to 6
- keys: bfloat16 [32768, 2048], P(('sec', 'grp')), may hold values from -6 to 6
- values: bfloat16 [32768, 2048], P(('sec', 'grp')), may hold values from -6 to 6
- dout: bfloat16 [32768, 2048], P(('sec', 'grp')), may hold values from -48 to 48
- history: bfloat16 [1024, 2, 2048], P('sec', None, 'grp'), may hold values from -6 to 6
- context: int32 [16], replicated, may hold values from 1 to 1024, as said below
Outputs:
- grad_queries: bfloat16 [32768, 2048], P(('sec', 'grp'))
- grad_keys: bfloat16 [32768, 2048], P(('sec', 'grp'))
- grad_values: bfloat16 [32768, 2048], P(('sec', 'grp'))
- grad_history: float32 [1024, 2, 2048], P('sec', None, 'grp')
The draws below stay inside these ranges and needn't reach their ends.
Inputs may be any that keep to these rules, and one draw needn't show every extreme that they name: Section s attends to history rows 0 to context[s] - 1; some section attends to all 1024 rows.
All inputs are finite; a program needn't handle non-finite values.
Results may differ from the reference program's by a relative error of at most 0.017.
Values may be sent and summed in bfloat16 or wider, within the bound.
A program may use at most 64 MiB of HBM per device.

```python
import jax
import jax.numpy as jnp
from jax import lax

HEADS = 16
HD = 128
SECTIONS = 16
SEC_TOK = 2048
TOKENS = 32768
HIST = 1024


def draw_queries(key, part):
    key = jax.random.fold_in(key, 1)
    base = jnp.clip(1.4 * jax.random.normal(key, (TOKENS, HEADS * HD), jnp.float32), -6.0, 6.0)
    return base.astype(jnp.bfloat16)


def draw_keys(key, part):
    key = jax.random.fold_in(key, 2)
    base = jnp.clip(1.4 * jax.random.normal(key, (TOKENS, HEADS * HD), jnp.float32), -6.0, 6.0)
    return base.astype(jnp.bfloat16)


def draw_context(key, part):
    key = jax.random.fold_in(key, 3)
    counts = jax.random.randint(jax.random.fold_in(key, 1), (SECTIONS,), 1, HIST + 1)
    full = jax.random.randint(jax.random.fold_in(key, 2), (), 0, SECTIONS)
    return jnp.where(jnp.arange(SECTIONS) == full, HIST, counts).astype(jnp.int32)


def level_of(rng, shape, split, least, high):
    def one(dim, shards_of):
        steps = jax.random.uniform(jax.random.fold_in(jax.random.fold_in(rng, 6), dim), (shards_of,), jnp.float32, least / len(split), high / len(split))
        return jnp.repeat(jnp.exp(steps), shape[dim] // shards_of).reshape((-1,) + (1,) * (len(shape) - dim - 1))

    level = one(*split[0])
    for cut in split[1:]:
        level = level * one(*cut)
    return level


def bell_draw(rng, extent, spread, most, split=(), kind=jnp.bfloat16):
    factor_of = level_of(rng, extent, split, -0.22, 0.18) if split else 1.0
    entries = jax.random.normal(rng, extent, jnp.float32) * spread * factor_of
    return jnp.minimum(jnp.maximum(entries, -most), most).astype(kind)


def setup_inputs(seed: int = 0) -> dict:
    streams_of = jax.random.split(jax.random.key(seed), 7)
    queries = draw_queries(jax.random.fold_in(streams_of[6], 71), 0)
    keys = draw_keys(jax.random.fold_in(streams_of[6], 71), 0)
    values = bell_draw(streams_of[2], (TOKENS, HEADS * HD), 1.0, 6.0, ((0, 256),))
    dout = bell_draw(streams_of[3], (TOKENS, HEADS * HD), 8.0, 48.0, ((0, 256),))
    history = bell_draw(streams_of[4], (HIST, 2, HEADS * HD), 1.4, 6.0, ((0, 16), (2, 16)))
    context = draw_context(jax.random.fold_in(streams_of[6], 71), 0)
    return {"queries": queries, "keys": keys, "values": values, "dout": dout, "history": history, "context": context}


def head_grad(q, k, v, g, hist_k, hist_v, ctx):
    scale = HD ** (-0.5)
    key_list = jnp.concatenate([k, hist_k], 0).astype(jnp.float32)
    val_list = jnp.concatenate([v, hist_v], 0).astype(jnp.float32)
    qf = q.astype(jnp.float32)
    gf = g.astype(jnp.float32)
    visible = jnp.arange(SEC_TOK + HIST, dtype=jnp.int32) < SEC_TOK + ctx
    scores = jnp.dot(qf, key_list.T) * scale
    scores = jnp.where(visible[None, :], scores, -jnp.inf)
    top = lax.optimization_barrier(jnp.max(scores, axis=-1, keepdims=True))
    lse = top + jnp.log(lax.optimization_barrier(jnp.sum(jnp.exp(scores - top), axis=-1, keepdims=True)))
    probs = jnp.exp(scores - lse)
    probs_low = lax.optimization_barrier(probs.astype(jnp.bfloat16)).astype(jnp.float32)
    out = jnp.dot(probs_low, val_list)
    delta = lax.optimization_barrier(jnp.sum(gf * out, axis=-1, keepdims=True))
    dprobs = jnp.dot(gf, val_list.T)
    dscores = lax.optimization_barrier((probs * (dprobs - delta) * scale).astype(jnp.bfloat16)).astype(jnp.float32)
    grad_q = jnp.dot(dscores, key_list).astype(jnp.bfloat16)
    key_terms = jnp.dot(dscores.T, qf)
    value_terms = jnp.dot(probs_low.T, gf)
    return (grad_q, key_terms[:SEC_TOK].astype(jnp.bfloat16), value_terms[:SEC_TOK].astype(jnp.bfloat16), key_terms[SEC_TOK:], value_terms[SEC_TOK:])

def reference(queries, keys, values, dout, history, context):
    hist_k = history[:, 0].reshape(HIST, HEADS, HD).transpose(1, 0, 2)
    hist_v = history[:, 1].reshape(HIST, HEADS, HD).transpose(1, 0, 2)

    def shaped(a):
        return a.reshape(SECTIONS, SEC_TOK, HEADS, HD).transpose(0, 2, 1, 3)

    def per_section(args):
        q, k, v, g, ctx = args

        def per_head(hargs):
            return head_grad(*hargs, ctx)
        return lax.map(per_head, (q, k, v, g, hist_k, hist_v))
    grad_q, grad_k, grad_v, hist_kt, hist_vt = lax.map(per_section, (shaped(queries), shaped(keys), shaped(values), shaped(dout), context))

    def unshaped(a):
        return a.transpose(0, 2, 1, 3).reshape(TOKENS, HEADS * HD)
    total_k = lax.optimization_barrier(jnp.sum(hist_kt, axis=0)).transpose(1, 0, 2).reshape(HIST, HEADS * HD)
    total_v = lax.optimization_barrier(jnp.sum(hist_vt, axis=0)).transpose(1, 0, 2).reshape(HIST, HEADS * HD)
    grad_history = jnp.stack([total_k, total_v], axis=1)
    return (unshaped(grad_q), unshaped(grad_k), unshaped(grad_v), grad_history)
```

```python
import functools
import math

import jax
import jax.numpy as jnp
from jax import lax
from jax.experimental import pallas as pl
from jax.experimental.pallas import tpu as pltpu
from jax.sharding import PartitionSpec as P

HD = 128
MESH = pl.DeviceIdType.MESH
NT = (((1,), (1,)), ((), ()))
NN = (((1,), (0,)), ((), ()))
F32 = jnp.float32
BF = jnp.bfloat16
SCALE = HD ** (-0.5)
LOG2E = math.log2(math.e)
KC = 512


def dot(a, b, dims=NN):
    return lax.dot_general(a, b, dims, preferred_element_type=F32)


def kernel(
    secs,
    grps,
    q_in,
    k_in,
    v_in,
    g_in,
    h_in,
    ctx_in,
    gq_out,
    gk_out,
    gv_out,
    gh_out,
    qb,
    gb,
    kb,
    vb,
    kt,
    sb,
    eb,
    db,
    dka,
    dva,
    dqs,
    dks,
    dvs,
    hbk,
    hbv,
    in_send,
    in_recv,
    h_send,
    h_recv,
    out_send,
    out_recv,
    gh_send,
    gh_recv,
):
    own = q_in.shape[0]
    chips = grps // 2
    block = 2 * own
    seq = grps * own
    hown = h_in.shape[0]
    keys = seq + secs * hown
    parts = keys // KC
    sec = lax.axis_index("sec")
    grp = lax.axis_index("grp")
    z, core = grp // 2, grp % 2

    def shift(t):
        return ((t + 1) // 2) * (2 * (t % 2) - 1) + chips

    def to_chip(t):
        return (z + shift(t)) % chips

    def from_chip(t):
        return (z - shift(t) + 2 * chips) % chips

    def device(chip, dc):
        return 2 * chip + (core + dc) % 2

    def cols(d):
        return pl.ds(pl.multiple_of(d * HD, HD), HD)

    def rows(d, n, base=0):
        return pl.ds(pl.multiple_of(base + d * n, n), n)

    barrier = pltpu.get_barrier_semaphore()

    @pl.loop(1, grps)
    def _(i):
        pl.semaphore_signal(
            barrier, 1, device_id=(sec, (grp + i) % grps), device_id_type=MESH
        )

    @pl.loop(1, secs)
    def _(i):
        pl.semaphore_signal(
            barrier, 1, device_id=((sec + i) % secs, grp), device_id_type=MESH
        )

    pl.semaphore_wait(barrier, grps + secs - 2)

    def in_copy(a, src, dst, t, dc):
        to = device(to_chip(t), dc)
        return pltpu.make_async_remote_copy(
            src.at[:, cols(to)],
            dst.at[rows(grp, own)],
            in_send.at[a, 2 * t + dc],
            in_recv.at[a, 2 * t + dc],
            device_id=(sec, to),
            device_id_type=MESH,
        )

    def in_local(a, src, dst):
        return pltpu.make_async_copy(
            src.at[:, cols(grp)], dst.at[rows(grp, own)], in_recv.at[a, 0]
        )

    arrays = ((0, k_in, kb), (1, v_in, vb), (2, q_in, qb), (3, g_in, gb))

    def h_copy(a, dst, i):
        return pltpu.make_async_remote_copy(
            h_in.at[:, pl.ds(a * HD, HD)],
            dst.at[rows(sec, hown, seq)],
            h_send.at[a, i],
            h_recv.at[a, i],
            device_id=((sec + i) % secs, grp),
            device_id_type=MESH,
        )

    def h_local(a, dst):
        return pltpu.make_async_copy(
            h_in.at[:, pl.ds(a * HD, HD)], dst.at[rows(sec, hown, seq)], h_recv.at[a, 0]
        )

    def start_in(first, last):
        for a, src, dst in arrays[first:last]:
            in_local(a, src, dst).start()
        for a, src, dst in arrays[first:last]:
            in_copy(a, src, dst, 0, 1).start()

        @pl.loop(1, chips)
        def _(t):
            for a, src, dst in arrays[first:last]:
                in_copy(a, src, dst, t, 0).start()
                in_copy(a, src, dst, t, 1).start()

    start_in(0, 2)
    for a, dst in ((0, kb), (1, vb)):
        h_local(a, dst).start()

    @pl.loop(1, secs)
    def _(i):
        h_copy(0, kb, i).start()
        h_copy(1, vb, i).start()

    start_in(2, 4)

    dka[...] = jnp.zeros_like(dka)
    dva[...] = jnp.zeros_like(dva)
    ctx = ctx_in[sec]

    def wait_in(a, src, dst, t, dc):
        if dc == 0:

            @pl.when(t == 0)
            def _():
                in_local(a, src, dst).wait()

            @pl.when(t > 0)
            def _():
                in_copy(a, src, dst, t, dc).wait_recv()
        else:
            in_copy(a, src, dst, t, dc).wait_recv()

    @pl.loop(0, chips)
    def _(t):
        for a, src, dst in arrays[:2]:
            for dc in range(2):
                wait_in(a, src, dst, t, dc)

    for a, dst in ((0, kb), (1, vb)):
        h_local(a, dst).wait()

    @pl.loop(1, secs)
    def _(i):
        h_copy(0, kb, i).wait_recv()
        h_copy(1, vb, i).wait_recv()

    for j in range(parts):
        kt[:, j * KC : (j + 1) * KC] = kb[j * KC : (j + 1) * KC, :].T

    def out_copy(a, src, dst, t, dc):
        to = device(from_chip(t), dc)
        return pltpu.make_async_remote_copy(
            src.at[rows(to, own)],
            dst.at[:, cols(grp)],
            out_send.at[a, 2 * t + dc],
            out_recv.at[a, 2 * t + dc],
            device_id=(sec, to),
            device_id_type=MESH,
        )

    def out_local(a, src, dst):
        return pltpu.make_async_copy(
            src.at[rows(grp, own)], dst.at[:, cols(grp)], out_recv.at[a, 0]
        )

    def start_out(a, src, dst, t):
        out_copy(a, src, dst, t, 1).start()

        @pl.when(t == 0)
        def _():
            out_local(a, src, dst).start()

        @pl.when(t > 0)
        def _():
            out_copy(a, src, dst, t, 0).start()

    @pl.loop(0, chips)
    def _(t):
        for a, src, dst in arrays[2:]:
            for dc in range(2):
                wait_in(a, src, dst, t, dc)
        here = rows(from_chip(t), block)
        q = qb[here, :]
        g = gb[here, :]
        top = jnp.full((8, block), -jnp.inf, F32)
        for j in range(parts):
            part = slice(j * KC, (j + 1) * KC)
            s = dot(kb[part, :], q, NT)
            if (j + 1) * KC > seq:
                row = lax.broadcasted_iota(jnp.int32, (KC, block), 0) + (j * KC - seq)
                s = jnp.where(row < ctx, s, -jnp.inf)
            sb[part, :] = s
            top = jnp.maximum(top, jnp.max(s.reshape(KC // 8, 8, block), axis=0))
        top = jnp.max(top, axis=0, keepdims=True)
        total = jnp.zeros((8, block), F32)
        delta = jnp.zeros((8, block), F32)
        for j in range(parts):
            part = slice(j * KC, (j + 1) * KC)
            e = jnp.exp2((sb[part, :] - top) * (SCALE * LOG2E))
            dp = dot(vb[part, :], g, NT)
            total = total + jnp.sum(e.reshape(KC // 8, 8, block), axis=0)
            delta = delta + jnp.sum((e * dp).reshape(KC // 8, 8, block), axis=0)
            eb[part, :] = e
            db[part, :] = dp
        inv = 1.0 / jnp.sum(total, axis=0, keepdims=True)
        delta = jnp.sum(delta, axis=0, keepdims=True) * inv
        inv_col = jnp.transpose(jnp.broadcast_to(inv, (HD, block)))
        gs = (g.astype(F32) * inv_col).astype(BF)
        qs = (q.astype(F32) * (inv_col * SCALE)).astype(BF)
        dqt = jnp.zeros((HD, block), F32)
        for j in range(parts):
            part = slice(j * KC, (j + 1) * KC)
            e = eb[part, :]
            ds = (e * (db[part, :] - delta)).astype(BF)
            dva[part, :] += dot(e.astype(BF), gs)
            dka[part, :] += dot(ds, qs)
            dqt = dqt + dot(kt[:, part], ds)
        dqs[here, :] = jnp.transpose(dqt * (inv * SCALE)).astype(BF)
        start_out(0, dqs, gq_out, t)

    def gh_copy(a, src, dst, i):
        to = (sec + i) % secs
        return pltpu.make_async_remote_copy(
            src.at[rows(to, hown, seq)],
            dst.at[rows(i, hown)],
            gh_send.at[a, i],
            gh_recv.at[a, i],
            device_id=(to, grp),
            device_id_type=MESH,
        )

    def gh_local(a, src, dst):
        return pltpu.make_async_copy(
            src.at[rows(sec, hown, seq)], dst.at[rows(0, hown)], gh_recv.at[a, 0]
        )

    hist_parts = ((0, dks, hbk), (1, dvs, hbv))
    dks[seq:, :] = dka[seq:, :].astype(BF)
    dvs[seq:, :] = dva[seq:, :].astype(BF)
    for a, src, dst in hist_parts:
        gh_local(a, src, dst).start()

    @pl.loop(1, secs)
    def _(i):
        for a, src, dst in hist_parts:
            gh_copy(a, src, dst, i).start()

    back = ((1, dks, gk_out), (2, dvs, gv_out))

    @pl.loop(0, chips)
    def _(t):
        here = rows(from_chip(t), block)
        dks[here, :] = dka[here, :].astype(BF)
        dvs[here, :] = dva[here, :].astype(BF)
        for a, src, dst in back:
            start_out(a, src, dst, t)

    for a, src, dst in hist_parts:
        gh_local(a, src, dst).wait()

    @pl.loop(1, secs)
    def _(i):
        for a, src, dst in hist_parts:
            gh_copy(a, src, dst, i).wait()

    for a, buf in ((0, hbk), (1, hbv)):
        acc = buf[0:hown, :].astype(F32)
        for i in range(1, secs):
            acc = acc + buf[i * hown : (i + 1) * hown, :].astype(F32)
        gh_out[:, a * HD : (a + 1) * HD] = acc

    @pl.loop(1, secs)
    def _(i):
        h_copy(0, kb, i).wait_send()
        h_copy(1, vb, i).wait_send()

    for a, src, dst in arrays:
        in_copy(a, src, dst, 0, 1).wait_send()
    for a, src, dst in ((0, dqs, gq_out),) + back:
        out_copy(a, src, dst, 0, 1).wait()
        out_local(a, src, dst).wait()

    @pl.loop(1, chips)
    def _(t):
        for dc in range(2):
            for a, src, dst in arrays:
                in_copy(a, src, dst, t, dc).wait_send()
            for a, src, dst in ((0, dqs, gq_out),) + back:
                out_copy(a, src, dst, t, dc).wait()


def on_device(secs, grps, queries, keys, values, dout, history, context):
    own = queries.shape[0]
    hown = history.shape[0]
    seq = own * grps
    total = seq + hown * secs
    block = 2 * own
    hist = history.reshape(hown, 2 * HD)
    anywhere = pl.BlockSpec(memory_space=pl.ANY)
    vmem = pl.BlockSpec(memory_space=pltpu.VMEM)
    smem = pl.BlockSpec(memory_space=pltpu.SMEM)
    dma = pltpu.SemaphoreType.DMA
    gq, gk, gv, gh = pl.pallas_call(
        functools.partial(kernel, secs, grps),
        out_shape=[
            jax.ShapeDtypeStruct(queries.shape, BF),
            jax.ShapeDtypeStruct(keys.shape, BF),
            jax.ShapeDtypeStruct(values.shape, BF),
            jax.ShapeDtypeStruct((hown, 2 * HD), F32),
        ],
        in_specs=[anywhere] * 5 + [smem],
        out_specs=[anywhere] * 3 + [vmem],
        scratch_shapes=[
            pltpu.VMEM((seq, HD), BF),
            pltpu.VMEM((seq, HD), BF),
            pltpu.VMEM((total, HD), BF),
            pltpu.VMEM((total, HD), BF),
            pltpu.VMEM((HD, total), BF),
            pltpu.VMEM((total, block), F32),
            pltpu.VMEM((total, block), F32),
            pltpu.VMEM((total, block), F32),
            pltpu.VMEM((total, HD), F32),
            pltpu.VMEM((total, HD), F32),
            pltpu.VMEM((seq, HD), BF),
            pltpu.VMEM((total, HD), BF),
            pltpu.VMEM((total, HD), BF),
            pltpu.VMEM((secs * hown, HD), BF),
            pltpu.VMEM((secs * hown, HD), BF),
            dma((4, grps)),
            dma((4, grps)),
            dma((2, secs)),
            dma((2, secs)),
            dma((3, grps)),
            dma((3, grps)),
            dma((2, secs)),
            dma((2, secs)),
        ],
        compiler_params=pltpu.CompilerParams(
            collective_id=0, has_side_effects=True, vmem_limit_bytes=40 * 2**20
        ),
    )(queries, keys, values, dout, hist, context)
    return gq, gk, gv, gh.reshape(hown, 2, HD)


def solution(mesh):
    secs, grps = mesh.shape["sec"], mesh.shape["grp"]
    split = P(("sec", "grp"), None)
    return jax.shard_map(
        functools.partial(on_device, secs, grps),
        mesh=mesh,
        in_specs=(split, split, split, split, P("sec", None, "grp"), P()),
        out_specs=(split, split, split, P("sec", None, "grp")),
        check_vma=False,
    )
```

```python
import functools
import math

import jax
import jax.numpy as jnp
from jax import lax
from jax.experimental import pallas as pl
from jax.experimental.pallas import tpu as pltpu
from jax.sharding import PartitionSpec as P

HD = 128
MESH = pl.DeviceIdType.MESH
NT = (((1,), (1,)), ((), ()))
NN = (((1,), (0,)), ((), ()))
F32 = jnp.float32
BF = jnp.bfloat16
SCALE = HD ** (-0.5)
LOG2E = math.log2(math.e)
KC = 512
VLIM = 58


def dot(a, b, dims=NN):
    return lax.dot_general(a, b, dims, preferred_element_type=F32)


def kernel(
    secs,
    grps,
    q_in,
    k_in,
    v_in,
    g_in,
    h_in,
    ctx_in,
    gq_out,
    gk_out,
    gv_out,
    gh_out,
    qb,
    gb,
    kb,
    vb,
    kt,
    sb,
    eb,
    db,
    dka,
    dva,
    dqs,
    dks,
    dvs,
    hb,
    hf,
    hgs,
    hgr,
    in_send,
    in_recv,
    h_send,
    h_recv,
    out_send,
    out_recv,
    gh_send,
    gh_recv,
    line_sem,
    go_sem,
):
    own = q_in.shape[0]
    chips = grps // 2
    block = 2 * own
    seq = grps * own
    hown = h_in.shape[0] // 2
    keys = seq + secs * hown
    parts = keys // KC
    sec = lax.axis_index("sec")
    grp = lax.axis_index("grp")
    z, core = grp // 2, grp % 2

    def shift(t):
        return ((t + 1) // 2) * (2 * (t % 2) - 1) + chips

    def to_chip(t):
        return (z + shift(t)) % chips

    def from_chip(t):
        return (z - shift(t) + 2 * chips) % chips

    def device(chip, dc):
        return 2 * chip + (core + dc) % 2

    def cols(d):
        return pl.ds(pl.multiple_of(d * HD, HD), HD)

    def rows(d, n, base=0):
        return pl.ds(pl.multiple_of(base + d * n, n), n)

    def in_copy(a, src, dst, t, dc):
        to = device(to_chip(t), dc)
        return pltpu.make_async_remote_copy(
            src.at[:, cols(to)],
            dst.at[rows(grp, own)],
            in_send.at[a, 2 * t + dc],
            in_recv.at[a, 2 * t + dc],
            device_id=(sec, to),
            device_id_type=MESH,
        )

    def in_local(a, src, dst):
        return pltpu.make_async_copy(
            src.at[:, cols(grp)], dst.at[rows(grp, own)], in_recv.at[a, 0]
        )

    arrays = ((0, k_in, kb), (1, v_in, vb), (2, q_in, qb), (3, g_in, gb))

    def h_copy(i):
        return pltpu.make_async_remote_copy(
            h_in,
            hb.at[rows(sec, 2 * hown)],
            h_send.at[i],
            h_recv.at[i],
            device_id=((sec + i) % secs, grp),
            device_id_type=MESH,
        )

    h_local = pltpu.make_async_copy(h_in, hb.at[rows(sec, 2 * hown)], h_recv.at[0])

    for a, src, dst in arrays:
        in_local(a, src, dst).start()
    h_local.start()

    beside = 2 * (chips // 2 + 1)
    leader = beside + 1
    barrier = pltpu.get_barrier_semaphore()

    @pl.loop(1, grps)
    def _(i):
        to = (grp + i) % grps

        @pl.when(to != leader)
        def _():
            pl.semaphore_signal(barrier, 1, device_id=(sec, to), device_id_type=MESH)

    @pl.when(grp != leader)
    def _():
        pl.semaphore_wait(barrier, grps - 1)

    @pl.when(grp == beside)
    def _():
        pl.semaphore_signal(line_sem, 1, device_id=(sec, leader), device_id_type=MESH)

    @pl.when(grp == leader)
    def _():
        pl.semaphore_wait(line_sem, 1)

        @pl.loop(1, secs)
        def _(i):
            pl.semaphore_signal(
                barrier, 1, device_id=((sec + i) % secs, grp), device_id_type=MESH
            )

    def all_there():
        @pl.when(grp == leader)
        def _():
            pl.semaphore_wait(barrier, secs - 1)

            @pl.loop(1, grps)
            def _(i):
                pl.semaphore_signal(
                    go_sem, 1, device_id=(sec, (grp + i) % grps), device_id_type=MESH
                )

        @pl.when(grp != leader)
        def _():
            pl.semaphore_wait(go_sem, 1)

    def start_in(first, last):
        for a, src, dst in arrays[first:last]:
            in_copy(a, src, dst, 0, 1).start()

        @pl.loop(1, chips)
        def _(t):
            for a, src, dst in arrays[first:last]:
                in_copy(a, src, dst, t, 0).start()
                in_copy(a, src, dst, t, 1).start()

    start_in(0, 1)
    all_there()

    @pl.loop(1, secs)
    def _(i):
        h_copy(i).start()

    start_in(1, 2)
    start_in(2, 4)

    dka[...] = jnp.zeros_like(dka)
    dva[...] = jnp.zeros_like(dva)
    ctx = ctx_in[sec]

    def wait_in(a, src, dst, t, dc):
        if dc == 0:

            @pl.when(t == 0)
            def _():
                in_local(a, src, dst).wait()

            @pl.when(t > 0)
            def _():
                in_copy(a, src, dst, t, dc).wait_recv()
        else:
            in_copy(a, src, dst, t, dc).wait_recv()

    h_local.wait()

    @pl.loop(1, secs)
    def _(i):
        h_copy(i).wait_recv()

    hist = secs * hown
    hf[...] = hb[...].astype(F32)
    kb[seq:, :] = hf[pl.ds(0, hist, stride=2), :].astype(BF)
    vb[seq:, :] = hf[pl.ds(1, hist, stride=2), :].astype(BF)

    @pl.loop(0, chips)
    def _(t):
        for a, src, dst in arrays[:2]:
            for dc in range(2):
                wait_in(a, src, dst, t, dc)

    for j in range(parts):
        kt[:, j * KC : (j + 1) * KC] = kb[j * KC : (j + 1) * KC, :].T

    def out_copy(a, src, dst, t, dc):
        to = device(from_chip(t), dc)
        return pltpu.make_async_remote_copy(
            src.at[rows(to, own)],
            dst.at[:, cols(grp)],
            out_send.at[a, 2 * t + dc],
            out_recv.at[a, 2 * t + dc],
            device_id=(sec, to),
            device_id_type=MESH,
        )

    def out_local(a, src, dst):
        return pltpu.make_async_copy(
            src.at[rows(grp, own)], dst.at[:, cols(grp)], out_recv.at[a, 0]
        )

    def start_out(a, src, dst, t):
        out_copy(a, src, dst, t, 1).start()

        @pl.when(t == 0)
        def _():
            out_local(a, src, dst).start()

        @pl.when(t > 0)
        def _():
            out_copy(a, src, dst, t, 0).start()

    @pl.loop(0, chips)
    def _(t):
        for a, src, dst in arrays[2:]:
            for dc in range(2):
                wait_in(a, src, dst, t, dc)
        here = rows(from_chip(t), block)
        q = qb[here, :]
        g = gb[here, :]
        top = jnp.full((8, block), -jnp.inf, F32)
        for j in range(parts):
            part = slice(j * KC, (j + 1) * KC)
            s = dot(kb[part, :], q, NT)
            if (j + 1) * KC > seq:
                row = lax.broadcasted_iota(jnp.int32, (KC, block), 0) + (j * KC - seq)
                s = jnp.where(row < ctx, s, -jnp.inf)
            sb[part, :] = s
            top = jnp.maximum(top, jnp.max(s.reshape(KC // 8, 8, block), axis=0))
        top = jnp.max(top, axis=0, keepdims=True)
        total = jnp.zeros((8, block), F32)
        delta = jnp.zeros((8, block), F32)
        for j in range(parts):
            part = slice(j * KC, (j + 1) * KC)
            e = jnp.exp2((sb[part, :] - top) * (SCALE * LOG2E))
            dp = dot(vb[part, :], g, NT)
            total = total + jnp.sum(e.reshape(KC // 8, 8, block), axis=0)
            delta = delta + jnp.sum((e * dp).reshape(KC // 8, 8, block), axis=0)
            eb[part, :] = e
            db[part, :] = dp
        inv = 1.0 / jnp.sum(total, axis=0, keepdims=True)
        delta = jnp.sum(delta, axis=0, keepdims=True) * inv
        inv_col = jnp.transpose(jnp.broadcast_to(inv, (HD, block)))
        gs = (g.astype(F32) * inv_col).astype(BF)
        qs = (q.astype(F32) * (inv_col * SCALE)).astype(BF)
        dqt = jnp.zeros((HD, block), F32)
        for j in range(parts):
            part = slice(j * KC, (j + 1) * KC)
            e = eb[part, :]
            ds = (e * (db[part, :] - delta)).astype(BF)
            dva[part, :] += dot(e.astype(BF), gs)
            dka[part, :] += dot(ds, qs)
            dqt = dqt + dot(kt[:, part], ds)
        dqs[here, :] = jnp.transpose(dqt * (inv * SCALE)).astype(BF)

        start_out(0, dqs, gq_out, t)

    def gh_copy(i):
        to = (sec + i) % secs
        return pltpu.make_async_remote_copy(
            hgs.at[rows(to, 2 * hown)],
            hgr.at[rows(i, 2 * hown)],
            gh_send.at[i],
            gh_recv.at[i],
            device_id=(to, grp),
            device_id_type=MESH,
        )

    gh_local = pltpu.make_async_copy(
        hgs.at[rows(sec, 2 * hown)], hgr.at[rows(0, 2 * hown)], gh_recv.at[0]
    )

    for i in range(secs):
        mine = slice(seq + i * hown, seq + (i + 1) * hown)
        hgs[2 * i * hown : (2 * i + 1) * hown, :] = dka[mine, :].astype(BF)
        hgs[(2 * i + 1) * hown : (2 * i + 2) * hown, :] = dva[mine, :].astype(BF)
    gh_local.start()

    @pl.loop(1, secs)
    def _(i):
        gh_copy(i).start()

    back = ((1, dks, gk_out), (2, dvs, gv_out))

    @pl.loop(0, chips)
    def _(t):
        here = rows(from_chip(t), block)
        dks[here, :] = dka[here, :].astype(BF)
        dvs[here, :] = dva[here, :].astype(BF)
        for a, src, dst in back:
            start_out(a, src, dst, t)

    gh_local.wait()

    @pl.loop(1, secs)
    def _(i):
        gh_copy(i).wait()

    acc = hgr[0 : 2 * hown, :].astype(F32)
    for i in range(1, secs):
        acc = acc + hgr[2 * i * hown : 2 * (i + 1) * hown, :].astype(F32)
    gh_out[pl.ds(0, hown, stride=2), :] = acc[:hown, :]
    gh_out[pl.ds(1, hown, stride=2), :] = acc[hown:, :]

    @pl.loop(1, secs)
    def _(i):
        h_copy(i).wait_send()

    for a, src, dst in arrays:
        in_copy(a, src, dst, 0, 1).wait_send()
    for a, src, dst in ((0, dqs, gq_out),) + back:
        out_copy(a, src, dst, 0, 1).wait()
        out_local(a, src, dst).wait()

    @pl.loop(1, chips)
    def _(t):
        for dc in range(2):
            for a, src, dst in arrays:
                in_copy(a, src, dst, t, dc).wait_send()
            for a, src, dst in ((0, dqs, gq_out),) + back:
                out_copy(a, src, dst, t, dc).wait()


def settle_kernel(n, *refs):
    ins, outs, held, sem = refs[:n], refs[n : 2 * n], refs[2 * n : 3 * n], refs[3 * n]
    arrive = [pltpu.make_async_copy(ins[i], held[i], sem.at[i]) for i in range(n)]
    leave = [pltpu.make_async_copy(held[i], outs[i], sem.at[n + i]) for i in range(n)]
    for copy in arrive:
        copy.start()
    for i in range(n):
        arrive[i].wait()
        leave[i].start()
    for copy in leave:
        copy.wait()


def settle(*arrays):
    n = len(arrays)
    anywhere = pl.BlockSpec(memory_space=pl.ANY)
    return pl.pallas_call(
        functools.partial(settle_kernel, n),
        out_shape=[jax.ShapeDtypeStruct(a.shape, a.dtype) for a in arrays],
        in_specs=[anywhere] * n,
        out_specs=[anywhere] * n,
        scratch_shapes=[pltpu.VMEM(a.shape, a.dtype) for a in arrays]
        + [pltpu.SemaphoreType.DMA((2 * n,))],
        compiler_params=pltpu.CompilerParams(vmem_limit_bytes=VLIM * 2**20),
    )(*arrays)


def on_device(secs, grps, queries, keys, values, dout, history, context):
    own = queries.shape[0]
    hown = history.shape[0]
    seq = own * grps
    total = seq + hown * secs
    block = 2 * own
    hist = history.reshape(2 * hown, HD)
    anywhere = pl.BlockSpec(memory_space=pl.ANY)
    vmem = pl.BlockSpec(memory_space=pltpu.VMEM)
    smem = pl.BlockSpec(memory_space=pltpu.SMEM)
    dma = pltpu.SemaphoreType.DMA
    gq, gk, gv, gh = pl.pallas_call(
        functools.partial(kernel, secs, grps),
        out_shape=[
            jax.ShapeDtypeStruct(queries.shape, BF),
            jax.ShapeDtypeStruct(keys.shape, BF),
            jax.ShapeDtypeStruct(values.shape, BF),
            jax.ShapeDtypeStruct((2 * hown, HD), F32),
        ],
        in_specs=[anywhere] * 5 + [smem],
        out_specs=[anywhere] * 3 + [vmem],
        scratch_shapes=[
            pltpu.VMEM((seq, HD), BF),
            pltpu.VMEM((seq, HD), BF),
            pltpu.VMEM((total, HD), BF),
            pltpu.VMEM((total, HD), BF),
            pltpu.VMEM((HD, total), BF),
            pltpu.VMEM((total, block), F32),
            pltpu.VMEM((total, block), F32),
            pltpu.VMEM((total, block), F32),
            pltpu.VMEM((total, HD), F32),
            pltpu.VMEM((total, HD), F32),
            pltpu.VMEM((seq, HD), BF),
            pltpu.VMEM((seq, HD), BF),
            pltpu.VMEM((seq, HD), BF),
            pltpu.VMEM((2 * secs * hown, HD), BF),
            pltpu.VMEM((2 * secs * hown, HD), F32),
            pltpu.VMEM((2 * secs * hown, HD), BF),
            pltpu.VMEM((2 * secs * hown, HD), BF),
            dma((4, grps)),
            dma((4, grps)),
            dma((secs,)),
            dma((secs,)),
            dma((3, grps)),
            dma((3, grps)),
            dma((secs,)),
            dma((secs,)),
            pltpu.SemaphoreType.REGULAR,
            pltpu.SemaphoreType.REGULAR,
        ],
        compiler_params=pltpu.CompilerParams(
            collective_id=0, has_side_effects=True, vmem_limit_bytes=VLIM * 2**20
        ),
    )(queries, keys, values, dout, hist, context)
    gq, gk, gv, gh = settle(gq, gk, gv, gh)
    return gq, gk, gv, gh.reshape(hown, 2, HD)


def solution(mesh):
    secs, grps = mesh.shape["sec"], mesh.shape["grp"]
    split = P(("sec", "grp"), None)
    return jax.shard_map(
        functools.partial(on_device, secs, grps),
        mesh=mesh,
        in_specs=(split, split, split, split, P("sec", None, "grp"), P()),
        out_specs=(split, split, split, P("sec", None, "grp")),
        check_vma=False,
    )
```

```python
import functools
import math

import jax
import jax.numpy as jnp
from jax import lax
from jax.experimental import pallas as pl
from jax.experimental.pallas import tpu as pltpu
from jax.sharding import PartitionSpec as P

HD = 128
MESH = pl.DeviceIdType.MESH
NT = (((1,), (1,)), ((), ()))
NN = (((1,), (0,)), ((), ()))
F32 = jnp.float32
BF = jnp.bfloat16
SCALE = HD ** (-0.5)
LOG2E = math.log2(math.e)
KC = 256
VLIM = 58


def dot(a, b, dims=NN):
    return lax.dot_general(a, b, dims, preferred_element_type=F32)


def kernel(
    secs,
    grps,
    q_in,
    k_in,
    v_in,
    g_in,
    h_in,
    ctx_in,
    gq_out,
    gk_out,
    gv_out,
    gh_out,
    qb,
    gb,
    kb,
    vb,
    kt,
    sb,
    eb,
    db,
    dka,
    dva,
    dqs,
    dks,
    dvs,
    hb,
    hf,
    hgs,
    hgr,
    in_send,
    in_recv,
    h_send,
    h_recv,
    out_send,
    out_recv,
    gh_send,
    gh_recv,
    line_sem,
    go_sem,
    ctx_all,
    ghs,
    own_sem,
):
    own = q_in.shape[0]
    chips = grps // 2
    block = 2 * own
    seq = grps * own
    hown = h_in.shape[0] // 2
    keys = seq + secs * hown
    parts = keys // KC
    sec = lax.axis_index("sec")
    grp = lax.axis_index("grp")
    z, core = grp // 2, grp % 2

    def shift(t):
        return ((t + 1) // 2) * (2 * (t % 2) - 1) + chips

    def turn(i):
        return i + ((i + 13) // 16) * (10 - 2 * i)

    def to_chip(t):
        return (z + shift(t)) % chips

    def from_chip(t):
        return (z - shift(t) + 2 * chips) % chips

    def device(chip, dc):
        return 2 * chip + (core + dc) % 2

    def cols(d):
        return pl.ds(pl.multiple_of(d * HD, HD), HD)

    def rows(d, n, base=0):
        return pl.ds(pl.multiple_of(base + d * n, n), n)

    def in_copy(a, src, dst, t, dc):
        to = device(to_chip(t), dc)
        return pltpu.make_async_remote_copy(
            src.at[:, cols(to)],
            dst.at[rows(grp, own)],
            in_send.at[a, 2 * t + dc],
            in_recv.at[a, 2 * t + dc],
            device_id=(sec, to),
            device_id_type=MESH,
        )

    def in_local(a, src, dst):
        return pltpu.make_async_copy(
            src.at[:, cols(grp)], dst.at[rows(grp, own)], in_recv.at[a, 0]
        )

    arrays = ((0, k_in, kb), (1, v_in, vb), (2, q_in, qb), (3, g_in, gb))

    def h_copy(i):
        return pltpu.make_async_remote_copy(
            h_in,
            hb.at[rows(sec, 2 * hown)],
            h_send.at[i],
            h_recv.at[i],
            device_id=((sec + i) % secs, grp),
            device_id_type=MESH,
        )

    h_local = pltpu.make_async_copy(h_in, hb.at[rows(sec, 2 * hown)], h_recv.at[0])

    beside = 2 * (chips // 2 + 1)
    leader = beside + 1
    barrier = pltpu.get_barrier_semaphore()
    for t in reversed(range(chips)):
        for dc in range(2):
            if t or dc:
                to = device(to_chip(t), dc)

                @pl.when(to != leader)
                def _(to=to):
                    pl.semaphore_signal(
                        barrier, 1, device_id=(sec, to), device_id_type=MESH
                    )

    for a, src, dst in arrays:
        in_local(a, src, dst).start()
    h_local.start()
    ctx_copy = pltpu.make_async_copy(ctx_in, ctx_all, own_sem.at[0])
    ctx_copy.start()
    gh_copy_out = pltpu.make_async_copy(ghs, gh_out, own_sem.at[1])

    @pl.when(grp != leader)
    def _():
        pl.semaphore_wait(barrier, grps - 1)

    @pl.when(grp == beside)
    def _():
        pl.semaphore_signal(line_sem, 1, device_id=(sec, leader), device_id_type=MESH)

    @pl.when(grp == leader)
    def _():
        pl.semaphore_wait(line_sem, 1)

        @pl.loop(1, secs)
        def _(i):
            pl.semaphore_signal(
                barrier, 1, device_id=((sec + i) % secs, grp), device_id_type=MESH
            )

    def all_there():
        @pl.when(grp == leader)
        def _():
            pl.semaphore_wait(barrier, secs - 1)

            @pl.loop(1, grps)
            def _(i):
                pl.semaphore_signal(
                    go_sem, 1, device_id=(sec, (grp + i) % grps), device_id_type=MESH
                )

        @pl.when(grp != leader)
        def _():
            pl.semaphore_wait(go_sem, 1)

    def start_in(first, last):
        for a, src, dst in arrays[first:last]:
            in_copy(a, src, dst, 0, 1).start()

        @pl.loop(1, chips)
        def _(i):
            t = turn(i)
            for a, src, dst in arrays[first:last]:
                in_copy(a, src, dst, t, 0).start()
                in_copy(a, src, dst, t, 1).start()

    start_in(0, 1)
    all_there()

    @pl.loop(1, secs)
    def _(i):
        h_copy(i).start()

    start_in(1, 2)
    start_in(2, 4)

    dka[...] = jnp.zeros_like(dka)
    dva[...] = jnp.zeros_like(dva)

    def wait_in(a, src, dst, t, dc):
        if dc == 0:

            @pl.when(t == 0)
            def _():
                in_local(a, src, dst).wait()

            @pl.when(t > 0)
            def _():
                in_copy(a, src, dst, t, dc).wait_recv()
        else:
            in_copy(a, src, dst, t, dc).wait_recv()

    h_local.wait()
    ctx_copy.wait()
    ctx = ctx_all[sec]

    @pl.loop(1, secs)
    def _(i):
        h_copy(i).wait_recv()

    hist = secs * hown
    hf[...] = hb[...].astype(F32)
    kb[seq:, :] = hf[pl.ds(0, hist, stride=2), :].astype(BF)
    vb[seq:, :] = hf[pl.ds(1, hist, stride=2), :].astype(BF)

    @pl.loop(0, chips)
    def _(t):
        for a, src, dst in arrays[:2]:
            for dc in range(2):
                wait_in(a, src, dst, t, dc)

    for j in range(parts):
        kt[:, j * KC : (j + 1) * KC] = kb[j * KC : (j + 1) * KC, :].T

    def out_copy(a, src, dst, t, dc):
        to = device(from_chip(t), dc)
        return pltpu.make_async_remote_copy(
            src.at[rows(to, own)],
            dst.at[:, cols(grp)],
            out_send.at[a, 2 * t + dc],
            out_recv.at[a, 2 * t + dc],
            device_id=(sec, to),
            device_id_type=MESH,
        )

    def out_local(a, src, dst):
        return pltpu.make_async_copy(
            src.at[rows(grp, own)], dst.at[:, cols(grp)], out_recv.at[a, 0]
        )

    def start_out(a, src, dst, t):
        out_copy(a, src, dst, t, 1).start()

        @pl.when(t == 0)
        def _():
            out_local(a, src, dst).start()

        @pl.when(t > 0)
        def _():
            out_copy(a, src, dst, t, 0).start()

    @pl.loop(0, chips)
    def _(i):
        t = turn(i)
        for a, src, dst in arrays[2:]:
            for dc in range(2):
                wait_in(a, src, dst, t, dc)
        here = rows(from_chip(t), block)
        q = qb[here, :]
        g = gb[here, :]
        top = jnp.full((8, block), -jnp.inf, F32)
        for j in range(parts):
            part = slice(j * KC, (j + 1) * KC)
            s = dot(kb[part, :], q, NT)
            if (j + 1) * KC > seq:
                row = lax.broadcasted_iota(jnp.int32, (KC, block), 0) + (j * KC - seq)
                s = jnp.where(row < ctx, s, -jnp.inf)
            sb[part, :] = s
            top = jnp.maximum(top, jnp.max(s.reshape(KC // 8, 8, block), axis=0))
        top = jnp.max(top, axis=0, keepdims=True)
        total = jnp.zeros((8, block), F32)
        delta = jnp.zeros((8, block), F32)
        for j in range(parts):
            part = slice(j * KC, (j + 1) * KC)
            e = jnp.exp2((sb[part, :] - top) * (SCALE * LOG2E))
            dp = dot(vb[part, :], g, NT)
            total = total + jnp.sum(e.reshape(KC // 8, 8, block), axis=0)
            delta = delta + jnp.sum((e * dp).reshape(KC // 8, 8, block), axis=0)
            eb[part, :] = e
            db[part, :] = dp
        inv = 1.0 / jnp.sum(total, axis=0, keepdims=True)
        delta = jnp.sum(delta, axis=0, keepdims=True) * inv
        inv_col = jnp.transpose(jnp.broadcast_to(inv, (HD, block)))
        gs = (g.astype(F32) * inv_col).astype(BF)
        qs = (q.astype(F32) * (inv_col * SCALE)).astype(BF)
        dqt = jnp.zeros((HD, block), F32)
        for j in range(parts):
            part = slice(j * KC, (j + 1) * KC)
            e = eb[part, :]
            ds = (e * (db[part, :] - delta)).astype(BF)
            dva[part, :] += dot(e.astype(BF), gs)
            dka[part, :] += dot(ds, qs)
            dqt = dqt + dot(kt[:, part], ds)
        dqs[here, :] = jnp.transpose(dqt * (inv * SCALE)).astype(BF)

        start_out(0, dqs, gq_out, t)

    def gh_copy(i):
        to = (sec + i) % secs
        return pltpu.make_async_remote_copy(
            hgs.at[rows(to, 2 * hown)],
            hgr.at[rows(i, 2 * hown)],
            gh_send.at[i],
            gh_recv.at[i],
            device_id=(to, grp),
            device_id_type=MESH,
        )

    gh_local = pltpu.make_async_copy(
        hgs.at[rows(sec, 2 * hown)], hgr.at[rows(0, 2 * hown)], gh_recv.at[0]
    )

    for i in range(secs):
        mine = slice(seq + i * hown, seq + (i + 1) * hown)
        hgs[2 * i * hown : (2 * i + 1) * hown, :] = dka[mine, :].astype(BF)
        hgs[(2 * i + 1) * hown : (2 * i + 2) * hown, :] = dva[mine, :].astype(BF)
    gh_local.start()

    @pl.loop(1, secs)
    def _(i):
        gh_copy(i).start()

    back = ((1, dks, gk_out), (2, dvs, gv_out))

    @pl.loop(0, chips)
    def _(i):
        t = chips - 1 - i
        here = rows(from_chip(t), block)
        dks[here, :] = dka[here, :].astype(BF)
        dvs[here, :] = dva[here, :].astype(BF)
        for a, src, dst in back:
            start_out(a, src, dst, t)

    gh_local.wait()

    @pl.loop(1, secs)
    def _(i):
        gh_copy(i).wait()

    acc = hgr[0 : 2 * hown, :].astype(F32)
    for i in range(1, secs):
        acc = acc + hgr[2 * i * hown : 2 * (i + 1) * hown, :].astype(F32)
    ghs[pl.ds(0, hown, stride=2), :] = acc[:hown, :]
    ghs[pl.ds(1, hown, stride=2), :] = acc[hown:, :]
    gh_copy_out.start()

    gh_copy_out.wait()

    @pl.loop(1, secs)
    def _(i):
        h_copy(i).wait_send()

    for a, src, dst in arrays:
        in_copy(a, src, dst, 0, 1).wait_send()
    out_copy(0, dqs, gq_out, 0, 1).wait()
    out_local(0, dqs, gq_out).wait()

    @pl.loop(1, chips)
    def _(i):
        t = turn(i)
        for dc in range(2):
            for a, src, dst in arrays:
                in_copy(a, src, dst, t, dc).wait_send()
            out_copy(0, dqs, gq_out, t, dc).wait()

    @pl.loop(1, chips)
    def _(i):
        for a, src, dst in back:
            for dc in range(2):
                out_copy(a, src, dst, chips - i, dc).wait()

    for a, src, dst in back:
        out_copy(a, src, dst, 0, 1).wait()
        out_local(a, src, dst).wait()


def settle_kernel(n, *refs):
    ins, outs, held, sem = refs[:n], refs[n : 2 * n], refs[2 * n : 3 * n], refs[3 * n]
    arrive = [pltpu.make_async_copy(ins[i], held[i], sem.at[i]) for i in range(n)]
    leave = [pltpu.make_async_copy(held[i], outs[i], sem.at[n + i]) for i in range(n)]
    for copy in arrive:
        copy.start()
    for i in range(n):
        arrive[i].wait()
        leave[i].start()
    for copy in leave:
        copy.wait()


def settle(*arrays):
    n = len(arrays)
    anywhere = pl.BlockSpec(memory_space=pl.ANY)
    return pl.pallas_call(
        functools.partial(settle_kernel, n),
        out_shape=[jax.ShapeDtypeStruct(a.shape, a.dtype) for a in arrays],
        in_specs=[anywhere] * n,
        out_specs=[anywhere] * n,
        scratch_shapes=[pltpu.VMEM(a.shape, a.dtype) for a in arrays]
        + [pltpu.SemaphoreType.DMA((2 * n,))],
        compiler_params=pltpu.CompilerParams(vmem_limit_bytes=VLIM * 2**20),
    )(*arrays)


def on_device(secs, grps, queries, keys, values, dout, history, context):
    own = queries.shape[0]
    hown = history.shape[0]
    seq = own * grps
    total = seq + hown * secs
    block = 2 * own
    hist = history.reshape(2 * hown, HD)
    anywhere = pl.BlockSpec(memory_space=pl.ANY)
    dma = pltpu.SemaphoreType.DMA
    gq, gk, gv, gh = pl.pallas_call(
        functools.partial(kernel, secs, grps),
        out_shape=[
            jax.ShapeDtypeStruct(queries.shape, BF),
            jax.ShapeDtypeStruct(keys.shape, BF),
            jax.ShapeDtypeStruct(values.shape, BF),
            jax.ShapeDtypeStruct((2 * hown, HD), F32),
        ],
        in_specs=[anywhere] * 6,
        out_specs=[anywhere] * 4,
        scratch_shapes=[
            pltpu.VMEM((seq, HD), BF),
            pltpu.VMEM((seq, HD), BF),
            pltpu.VMEM((total, HD), BF),
            pltpu.VMEM((total, HD), BF),
            pltpu.VMEM((HD, total), BF),
            pltpu.VMEM((total, block), F32),
            pltpu.VMEM((total, block), F32),
            pltpu.VMEM((total, block), F32),
            pltpu.VMEM((total, HD), F32),
            pltpu.VMEM((total, HD), F32),
            pltpu.VMEM((seq, HD), BF),
            pltpu.VMEM((seq, HD), BF),
            pltpu.VMEM((seq, HD), BF),
            pltpu.VMEM((2 * secs * hown, HD), BF),
            pltpu.VMEM((2 * secs * hown, HD), F32),
            pltpu.VMEM((2 * secs * hown, HD), BF),
            pltpu.VMEM((2 * secs * hown, HD), BF),
            dma((4, grps)),
            dma((4, grps)),
            dma((secs,)),
            dma((secs,)),
            dma((3, grps)),
            dma((3, grps)),
            dma((secs,)),
            dma((secs,)),
            pltpu.SemaphoreType.REGULAR,
            pltpu.SemaphoreType.REGULAR,
            pltpu.SMEM((secs,), jnp.int32),
            pltpu.VMEM((2 * hown, HD), F32),
            dma((2,)),
        ],
        compiler_params=pltpu.CompilerParams(
            collective_id=0, has_side_effects=True, vmem_limit_bytes=VLIM * 2**20
        ),
    )(queries, keys, values, dout, hist, context)
    gq, gk, gv, gh = settle(gq, gk, gv, gh)
    return gq, gk, gv, gh.reshape(hown, 2, HD)


def solution(mesh):
    secs, grps = mesh.shape["sec"], mesh.shape["grp"]
    split = P(("sec", "grp"), None)
    return jax.shard_map(
        functools.partial(on_device, secs, grps),
        mesh=mesh,
        in_specs=(split, split, split, split, P("sec", None, "grp"), P()),
        out_specs=(split, split, split, P("sec", None, "grp")),
        check_vma=False,
    )
```

```python
import functools
import math

import jax
import jax.numpy as jnp
from jax import lax
from jax.experimental import pallas as pl
from jax.experimental.pallas import tpu as pltpu
from jax.sharding import PartitionSpec as P

HD = 128
MESH = pl.DeviceIdType.MESH
NT = (((1,), (1,)), ((), ()))
NN = (((1,), (0,)), ((), ()))
F32 = jnp.float32
BF = jnp.bfloat16
SCALE = HD ** (-0.5)
LOG2E = math.log2(math.e)
KC = 256
VLIM = 48


def dot(a, b, dims=NN):
    return lax.dot_general(a, b, dims, preferred_element_type=F32)


def kernel(
    secs,
    grps,
    q_in,
    k_in,
    v_in,
    g_in,
    h_in,
    ctx_in,
    gq_out,
    gk_out,
    gv_out,
    gh_out,
    qb,
    gb,
    kb,
    vb,
    kt,
    sb,
    eb,
    db,
    dka,
    dva,
    dqs,
    dks,
    dvs,
    hb,
    hf,
    hgs,
    hgr,
    in_send,
    in_recv,
    h_send,
    h_recv,
    out_send,
    out_recv,
    gh_send,
    gh_recv,
    line_sem,
    go_sem,
    ctx_all,
    ghs,
    own_sem,
):
    own = q_in.shape[0]
    chips = grps // 2
    block = 2 * own
    seq = grps * own
    hown = h_in.shape[0] // 2
    keys = seq + secs * hown
    parts = keys // KC
    sec = lax.axis_index("sec")
    grp = lax.axis_index("grp")
    z, core = grp // 2, grp % 2

    def shift(t):
        return ((t + 1) // 2) * (2 * (t % 2) - 1) + chips

    def turn(i):
        return i + ((i + 13) // 16) * (10 - 2 * i)

    def to_chip(t):
        return (z + shift(t)) % chips

    def from_chip(t):
        return (z - shift(t) + 2 * chips) % chips

    def device(chip, dc):
        return 2 * chip + (core + dc) % 2

    def cols(d):
        return pl.ds(pl.multiple_of(d * HD, HD), HD)

    def rows(d, n, base=0):
        return pl.ds(pl.multiple_of(base + d * n, n), n)

    def in_copy(a, src, dst, t, dc):
        to = device(to_chip(t), dc)
        return pltpu.make_async_remote_copy(
            src.at[:, cols(to)],
            dst.at[rows(grp, own)],
            in_send.at[a, 2 * t + dc],
            in_recv.at[a, 2 * t + dc],
            device_id=(sec, to),
            device_id_type=MESH,
        )

    def in_local(a, src, dst):
        return pltpu.make_async_copy(
            src.at[:, cols(grp)], dst.at[rows(grp, own)], in_recv.at[a, 0]
        )

    arrays = ((0, k_in, kb), (1, v_in, vb), (2, q_in, qb), (3, g_in, gb))

    def h_copy(i):
        return pltpu.make_async_remote_copy(
            h_in,
            hb.at[rows(sec, 2 * hown)],
            h_send.at[i],
            h_recv.at[i],
            device_id=((sec + i) % secs, grp),
            device_id_type=MESH,
        )

    h_local = pltpu.make_async_copy(h_in, hb.at[rows(sec, 2 * hown)], h_recv.at[0])

    beside = 2 * (chips // 2 + 1)
    leader = beside + 1
    barrier = pltpu.get_barrier_semaphore()
    for t in reversed(range(chips)):
        for dc in range(2):
            if t or dc:
                to = device(to_chip(t), dc)

                @pl.when(to != leader)
                def _(to=to):
                    pl.semaphore_signal(
                        barrier, 1, device_id=(sec, to), device_id_type=MESH
                    )

    for a, src, dst in arrays:
        in_local(a, src, dst).start()
    h_local.start()
    ctx_copy = pltpu.make_async_copy(ctx_in, ctx_all, own_sem.at[0])
    ctx_copy.start()
    gh_copy_out = pltpu.make_async_copy(ghs, gh_out, own_sem.at[1])

    @pl.when(grp != leader)
    def _():
        pl.semaphore_wait(barrier, grps - 1)

    @pl.when(grp == beside)
    def _():
        pl.semaphore_signal(line_sem, 1, device_id=(sec, leader), device_id_type=MESH)

    @pl.when(grp == leader)
    def _():
        pl.semaphore_wait(line_sem, 1)

        @pl.loop(1, secs)
        def _(i):
            pl.semaphore_signal(
                barrier, 1, device_id=((sec + i) % secs, grp), device_id_type=MESH
            )

    def all_there():
        @pl.when(grp == leader)
        def _():
            pl.semaphore_wait(barrier, secs - 1)

            @pl.loop(1, grps)
            def _(i):
                pl.semaphore_signal(
                    go_sem, 1, device_id=(sec, (grp + i) % grps), device_id_type=MESH
                )

        @pl.when(grp != leader)
        def _():
            pl.semaphore_wait(go_sem, 1)

    def start_in(first, last):
        for a, src, dst in arrays[first:last]:
            in_copy(a, src, dst, 0, 1).start()

        @pl.loop(1, chips)
        def _(i):
            t = turn(i)
            for a, src, dst in arrays[first:last]:
                in_copy(a, src, dst, t, 0).start()
                in_copy(a, src, dst, t, 1).start()

    start_in(0, 1)
    all_there()

    @pl.loop(1, secs)
    def _(i):
        h_copy(i).start()

    start_in(1, 2)
    start_in(2, 4)

    dka[...] = jnp.zeros_like(dka)
    dva[...] = jnp.zeros_like(dva)

    def wait_in(a, src, dst, t, dc):
        if dc == 0:

            @pl.when(t == 0)
            def _():
                in_local(a, src, dst).wait()

            @pl.when(t > 0)
            def _():
                in_copy(a, src, dst, t, dc).wait_recv()
        else:
            in_copy(a, src, dst, t, dc).wait_recv()

    h_local.wait()
    ctx_copy.wait()
    ctx = ctx_all[sec]

    @pl.loop(1, secs)
    def _(i):
        h_copy(i).wait_recv()

    hist = secs * hown
    hf[...] = hb[...].astype(F32)
    kb[seq:, :] = hf[pl.ds(0, hist, stride=2), :].astype(BF)
    vb[seq:, :] = hf[pl.ds(1, hist, stride=2), :].astype(BF)

    @pl.loop(0, chips)
    def _(t):
        for a, src, dst in arrays[:2]:
            for dc in range(2):
                wait_in(a, src, dst, t, dc)

    for j in range(parts):
        kt[:, j * KC : (j + 1) * KC] = kb[j * KC : (j + 1) * KC, :].T

    def out_copy(a, src, dst, t, dc):
        to = device(from_chip(t), dc)
        return pltpu.make_async_remote_copy(
            src.at[rows(to, own)],
            dst.at[:, cols(grp)],
            out_send.at[a, 2 * t + dc],
            out_recv.at[a, 2 * t + dc],
            device_id=(sec, to),
            device_id_type=MESH,
        )

    def out_local(a, src, dst):
        return pltpu.make_async_copy(
            src.at[rows(grp, own)], dst.at[:, cols(grp)], out_recv.at[a, 0]
        )

    def start_out(a, src, dst, t):
        out_copy(a, src, dst, t, 1).start()

        @pl.when(t == 0)
        def _():
            out_local(a, src, dst).start()

        @pl.when(t > 0)
        def _():
            out_copy(a, src, dst, t, 0).start()

    @pl.loop(0, chips)
    def _(i):
        t = turn(i)
        for a, src, dst in arrays[2:]:
            for dc in range(2):
                wait_in(a, src, dst, t, dc)
        here = rows(from_chip(t), block)
        q = qb[here, :]
        g = gb[here, :]
        top = jnp.full((8, block), -jnp.inf, F32)
        for j in range(parts):
            part = slice(j * KC, (j + 1) * KC)
            s = dot(kb[part, :], q, NT)
            if (j + 1) * KC > seq:
                row = lax.broadcasted_iota(jnp.int32, (KC, block), 0) + (j * KC - seq)
                s = jnp.where(row < ctx, s, -jnp.inf)
            sb[part, :] = s
            top = jnp.maximum(top, jnp.max(s.reshape(KC // 8, 8, block), axis=0))
        top = jnp.max(top, axis=0, keepdims=True)
        total = jnp.zeros((8, block), F32)
        delta = jnp.zeros((8, block), F32)
        for j in range(parts):
            part = slice(j * KC, (j + 1) * KC)
            e = jnp.exp2((sb[part, :] - top) * (SCALE * LOG2E))
            dp = dot(vb[part, :], g, NT)
            total = total + jnp.sum(e.reshape(KC // 8, 8, block), axis=0)
            delta = delta + jnp.sum((e * dp).reshape(KC // 8, 8, block), axis=0)
            eb[part, :] = e
            db[part, :] = dp
        inv = 1.0 / jnp.sum(total, axis=0, keepdims=True)
        delta = jnp.sum(delta, axis=0, keepdims=True) * inv
        inv_col = jnp.transpose(jnp.broadcast_to(inv, (HD, block)))
        gs = (g.astype(F32) * inv_col).astype(BF)
        qs = (q.astype(F32) * (inv_col * SCALE)).astype(BF)
        dqt = jnp.zeros((HD, block), F32)
        for j in range(parts):
            part = slice(j * KC, (j + 1) * KC)
            e = eb[part, :]
            ds = (e * (db[part, :] - delta)).astype(BF)
            dva[part, :] += dot(e.astype(BF), gs)
            dka[part, :] += dot(ds, qs)
            dqt = dqt + dot(kt[:, part], ds)
        dqs[here, :] = jnp.transpose(dqt * (inv * SCALE)).astype(BF)

        start_out(0, dqs, gq_out, t)

    def gh_copy(i):
        to = (sec + i) % secs
        return pltpu.make_async_remote_copy(
            hgs.at[rows(to, 2 * hown)],
            hgr.at[rows(i, 2 * hown)],
            gh_send.at[i],
            gh_recv.at[i],
            device_id=(to, grp),
            device_id_type=MESH,
        )

    gh_local = pltpu.make_async_copy(
        hgs.at[rows(sec, 2 * hown)], hgr.at[rows(0, 2 * hown)], gh_recv.at[0]
    )

    for i in range(secs):
        mine = slice(seq + i * hown, seq + (i + 1) * hown)
        hgs[2 * i * hown : (2 * i + 1) * hown, :] = dka[mine, :].astype(BF)
        hgs[(2 * i + 1) * hown : (2 * i + 2) * hown, :] = dva[mine, :].astype(BF)
    gh_local.start()

    @pl.loop(1, secs)
    def _(i):
        gh_copy(i).start()

    back = ((1, dks, gk_out), (2, dvs, gv_out))

    @pl.loop(0, chips)
    def _(i):
        t = chips - 1 - i
        here = rows(from_chip(t), block)
        dks[here, :] = dka[here, :].astype(BF)
        dvs[here, :] = dva[here, :].astype(BF)
        for a, src, dst in back:
            start_out(a, src, dst, t)

    gh_local.wait()

    @pl.loop(1, secs)
    def _(i):
        gh_copy(i).wait()

    acc = hgr[0 : 2 * hown, :].astype(F32)
    for i in range(1, secs):
        acc = acc + hgr[2 * i * hown : 2 * (i + 1) * hown, :].astype(F32)
    ghs[pl.ds(0, hown, stride=2), :] = acc[:hown, :]
    ghs[pl.ds(1, hown, stride=2), :] = acc[hown:, :]
    gh_copy_out.start()

    gh_copy_out.wait()

    @pl.loop(1, secs)
    def _(i):
        h_copy(i).wait_send()

    for a, src, dst in arrays:
        in_copy(a, src, dst, 0, 1).wait_send()
    out_copy(0, dqs, gq_out, 0, 1).wait()
    out_local(0, dqs, gq_out).wait()

    @pl.loop(1, chips)
    def _(i):
        t = turn(i)
        for dc in range(2):
            for a, src, dst in arrays:
                in_copy(a, src, dst, t, dc).wait_send()
            out_copy(0, dqs, gq_out, t, dc).wait()

    @pl.loop(1, chips)
    def _(i):
        for a, src, dst in back:
            for dc in range(2):
                out_copy(a, src, dst, chips - i, dc).wait()

    for a, src, dst in back:
        out_copy(a, src, dst, 0, 1).wait()
        out_local(a, src, dst).wait()


def settle_kernel(n, *refs):
    ins, outs, sem = refs[:n], refs[n : 2 * n], refs[2 * n]
    copies = [pltpu.make_async_copy(ins[i], outs[i], sem.at[i]) for i in range(n)]
    for copy in copies:
        copy.start()
    for copy in copies:
        copy.wait()


def settle(*arrays):
    n = len(arrays)
    anywhere = pl.BlockSpec(memory_space=pl.ANY)
    return pl.pallas_call(
        functools.partial(settle_kernel, n),
        out_shape=[jax.ShapeDtypeStruct(a.shape, a.dtype) for a in arrays],
        in_specs=[anywhere] * n,
        out_specs=[anywhere] * n,
        scratch_shapes=[pltpu.SemaphoreType.DMA((n,))],
        compiler_params=pltpu.CompilerParams(vmem_limit_bytes=8 * 2**20),
    )(*[pltpu.with_memory_space_constraint(a, pltpu.VMEM) for a in arrays])


def on_device(secs, grps, queries, keys, values, dout, history, context):
    own = queries.shape[0]
    hown = history.shape[0]
    seq = own * grps
    total = seq + hown * secs
    block = 2 * own
    hist = history.reshape(2 * hown, HD)
    anywhere = pl.BlockSpec(memory_space=pl.ANY)
    dma = pltpu.SemaphoreType.DMA
    args = (queries, keys, values, dout, hist, context)
    gq, gk, gv, gh = pl.pallas_call(
        functools.partial(kernel, secs, grps),
        out_shape=[
            pltpu.VMEM(queries.shape, BF),
            pltpu.VMEM(keys.shape, BF),
            pltpu.VMEM(values.shape, BF),
            pltpu.VMEM((2 * hown, HD), F32),
        ],
        in_specs=[anywhere] * 6,
        out_specs=[pl.BlockSpec(memory_space=pltpu.VMEM)] * 4,
        scratch_shapes=[
            pltpu.VMEM((seq, HD), BF),
            pltpu.VMEM((seq, HD), BF),
            pltpu.VMEM((total, HD), BF),
            pltpu.VMEM((total, HD), BF),
            pltpu.VMEM((HD, total), BF),
            pltpu.VMEM((total, block), F32),
            pltpu.VMEM((total, block), F32),
            pltpu.VMEM((total, block), F32),
            pltpu.VMEM((total, HD), F32),
            pltpu.VMEM((total, HD), F32),
            pltpu.VMEM((seq, HD), BF),
            pltpu.VMEM((seq, HD), BF),
            pltpu.VMEM((seq, HD), BF),
            pltpu.VMEM((2 * secs * hown, HD), BF),
            pltpu.VMEM((2 * secs * hown, HD), F32),
            pltpu.VMEM((2 * secs * hown, HD), BF),
            pltpu.VMEM((2 * secs * hown, HD), BF),
            dma((4, grps)),
            dma((4, grps)),
            dma((secs,)),
            dma((secs,)),
            dma((3, grps)),
            dma((3, grps)),
            dma((secs,)),
            dma((secs,)),
            pltpu.SemaphoreType.REGULAR,
            pltpu.SemaphoreType.REGULAR,
            pltpu.SMEM((secs,), jnp.int32),
            pltpu.VMEM((2 * hown, HD), F32),
            dma((2,)),
        ],
        compiler_params=pltpu.CompilerParams(
            collective_id=0, has_side_effects=True, vmem_limit_bytes=VLIM * 2**20
        ),
    )(*[pltpu.with_memory_space_constraint(a, pltpu.HBM) for a in args])
    gq, gk, gv, gh = settle(gq, gk, gv, gh)
    return gq, gk, gv, gh.reshape(hown, 2, HD)


def solution(mesh):
    secs, grps = mesh.shape["sec"], mesh.shape["grp"]
    split = P(("sec", "grp"), None)
    return jax.shard_map(
        functools.partial(on_device, secs, grps),
        mesh=mesh,
        in_specs=(split, split, split, split, P("sec", None, "grp"), P()),
        out_specs=(split, split, split, P("sec", None, "grp")),
        check_vma=False,
    )
```

```python
import functools
import math

import jax
import jax.numpy as jnp
from jax import lax
from jax.experimental import pallas as pl
from jax.experimental.pallas import tpu as pltpu
from jax.sharding import PartitionSpec as P

HD = 128
MESH = pl.DeviceIdType.MESH
NT = (((1,), (1,)), ((), ()))
NN = (((1,), (0,)), ((), ()))
F32 = jnp.float32
BF = jnp.bfloat16
SCALE = HD ** (-0.5)
LOG2E = math.log2(math.e)
KC = 256
VLIM = 48


def dot(a, b, dims=NN):
    return lax.dot_general(a, b, dims, preferred_element_type=F32)


def kernel(
    secs,
    grps,
    q_in,
    k_in,
    v_in,
    g_in,
    h_in,
    ctx_in,
    gq_out,
    gk_out,
    gv_out,
    gh_out,
    qb,
    gb,
    kb,
    vb,
    kt,
    sb,
    eb,
    db,
    dka,
    dva,
    dqs,
    dks,
    dvs,
    hb,
    hf,
    hgs,
    hgr,
    in_send,
    in_recv,
    h_send,
    h_recv,
    out_send,
    out_recv,
    gh_send,
    gh_recv,
    line_sem,
    go_sem,
    near_sem,
    ctx_all,
    ghs,
    own_sem,
):
    own = q_in.shape[0]
    chips = grps // 2
    block = 2 * own
    seq = grps * own
    hown = h_in.shape[0] // 2
    keys = seq + secs * hown
    parts = keys // KC
    sec = lax.axis_index("sec")
    grp = lax.axis_index("grp")
    z, core = grp // 2, grp % 2

    def shift(t):
        return ((t + 1) // 2) * (2 * (t % 2) - 1) + chips

    def turn(i):
        return i + ((i + 13) // 16) * (10 - 2 * i)

    def to_chip(t):
        return (z + shift(t)) % chips

    def from_chip(t):
        return (z - shift(t) + 2 * chips) % chips

    def device(chip, dc):
        return 2 * chip + (core + dc) % 2

    def cols(d):
        return pl.ds(pl.multiple_of(d * HD, HD), HD)

    def rows(d, n, base=0):
        return pl.ds(pl.multiple_of(base + d * n, n), n)

    def in_copy(a, src, dst, t, dc):
        to = device(to_chip(t), dc)
        return pltpu.make_async_remote_copy(
            src.at[:, cols(to)],
            dst.at[rows(grp, own)],
            in_send.at[a, 2 * t + dc],
            in_recv.at[a, 2 * t + dc],
            device_id=(sec, to),
            device_id_type=MESH,
        )

    def in_local(a, src, dst):
        return pltpu.make_async_copy(
            src.at[:, cols(grp)], dst.at[rows(grp, own)], in_recv.at[a, 0]
        )

    arrays = ((0, k_in, kb), (1, v_in, vb), (2, q_in, qb), (3, g_in, gb))

    def h_copy(i):
        return pltpu.make_async_remote_copy(
            h_in,
            hb.at[rows(sec, 2 * hown)],
            h_send.at[i],
            h_recv.at[i],
            device_id=((sec + i) % secs, grp),
            device_id_type=MESH,
        )

    h_local = pltpu.make_async_copy(h_in, hb.at[rows(sec, 2 * hown)], h_recv.at[0])

    beside = 2 * (chips // 2 + 1)
    leader = beside + 1
    barrier = pltpu.get_barrier_semaphore()
    for t, dc in ((0, 1), (1, 0), (1, 1), (2, 0), (2, 1)):
        to = device(to_chip(t), dc)

        @pl.when(to != leader)
        def _(to=to):
            pl.semaphore_signal(barrier, 1, device_id=(sec, to), device_id_type=MESH)

    for a, src, dst in arrays:
        in_local(a, src, dst).start()
    h_local.start()
    ctx_copy = pltpu.make_async_copy(ctx_in, ctx_all, own_sem.at[0])
    ctx_copy.start()
    gh_copy_out = pltpu.make_async_copy(ghs, gh_out, own_sem.at[1])

    @pl.when(grp != leader)
    def _():
        pl.semaphore_wait(barrier, 5)

    @pl.when(grp == beside)
    def _():
        pl.semaphore_signal(line_sem, 1, device_id=(sec, leader), device_id_type=MESH)

    @pl.when(grp == leader)
    def _():
        pl.semaphore_wait(line_sem, 1)

    def tell(r):
        for t in (1, 2):
            pl.semaphore_signal(
                near_sem.at[r],
                1,
                device_id=(sec, device(to_chip(t), 0)),
                device_id_type=MESH,
            )

    def hear(r):
        pl.semaphore_wait(near_sem.at[r], 2)

    def meet():
        @pl.when(grp == leader)
        def _():
            @pl.loop(1, secs)
            def _(i):
                pl.semaphore_signal(
                    barrier, 1, device_id=((sec + i) % secs, grp), device_id_type=MESH
                )

    def all_there():
        @pl.when(grp == leader)
        def _():
            pl.semaphore_wait(barrier, secs - 1)

            @pl.loop(1, grps)
            def _(i):
                pl.semaphore_signal(
                    go_sem, 1, device_id=(sec, (grp + i) % grps), device_id_type=MESH
                )

        @pl.when(grp != leader)
        def _():
            pl.semaphore_wait(go_sem, 1)

    def start_in(first, last):
        for a, src, dst in arrays[first:last]:
            in_copy(a, src, dst, 0, 1).start()

        @pl.loop(1, chips)
        def _(i):
            t = turn(i)
            for a, src, dst in arrays[first:last]:
                in_copy(a, src, dst, t, 0).start()
                in_copy(a, src, dst, t, 1).start()

    tell(0)
    for a, src, dst in arrays[:2]:
        in_copy(a, src, dst, 0, 1).start()
    for step in range(chips // 2):
        for t in (2 * step + 1, 2 * step + 2):
            if t < chips:
                for a, src, dst in arrays[:2]:
                    in_copy(a, src, dst, t, 0).start()
                    in_copy(a, src, dst, t, 1).start()
        if step < chips // 2 - 1:
            hear(step)
            if step < chips // 2 - 2:
                tell(step + 1)
    meet()
    all_there()

    @pl.loop(1, secs)
    def _(i):
        h_copy(i).start()

    start_in(2, 4)

    dka[...] = jnp.zeros_like(dka)
    dva[...] = jnp.zeros_like(dva)

    def wait_in(a, src, dst, t, dc):
        if dc == 0:

            @pl.when(t == 0)
            def _():
                in_local(a, src, dst).wait()

            @pl.when(t > 0)
            def _():
                in_copy(a, src, dst, t, dc).wait_recv()
        else:
            in_copy(a, src, dst, t, dc).wait_recv()

    h_local.wait()
    ctx_copy.wait()
    ctx = ctx_all[sec]

    @pl.loop(1, secs)
    def _(i):
        h_copy(i).wait_recv()

    hist = secs * hown
    hf[...] = hb[...].astype(F32)
    kb[seq:, :] = hf[pl.ds(0, hist, stride=2), :].astype(BF)
    vb[seq:, :] = hf[pl.ds(1, hist, stride=2), :].astype(BF)

    @pl.loop(0, chips)
    def _(t):
        for a, src, dst in arrays[:2]:
            for dc in range(2):
                wait_in(a, src, dst, t, dc)

    for j in range(parts):
        kt[:, j * KC : (j + 1) * KC] = kb[j * KC : (j + 1) * KC, :].T

    def out_copy(a, src, dst, t, dc):
        to = device(from_chip(t), dc)
        return pltpu.make_async_remote_copy(
            src.at[rows(to, own)],
            dst.at[:, cols(grp)],
            out_send.at[a, 2 * t + dc],
            out_recv.at[a, 2 * t + dc],
            device_id=(sec, to),
            device_id_type=MESH,
        )

    def out_local(a, src, dst):
        return pltpu.make_async_copy(
            src.at[rows(grp, own)], dst.at[:, cols(grp)], out_recv.at[a, 0]
        )

    def start_out(a, src, dst, t):
        out_copy(a, src, dst, t, 1).start()

        @pl.when(t == 0)
        def _():
            out_local(a, src, dst).start()

        @pl.when(t > 0)
        def _():
            out_copy(a, src, dst, t, 0).start()

    @pl.loop(0, chips)
    def _(i):
        t = turn(i)
        for a, src, dst in arrays[2:]:
            for dc in range(2):
                wait_in(a, src, dst, t, dc)
        here = rows(from_chip(t), block)
        q = qb[here, :]
        g = gb[here, :]
        top = jnp.full((8, block), -jnp.inf, F32)
        for j in range(parts):
            part = slice(j * KC, (j + 1) * KC)
            s = dot(kb[part, :], q, NT)
            if (j + 1) * KC > seq:
                row = lax.broadcasted_iota(jnp.int32, (KC, block), 0) + (j * KC - seq)
                s = jnp.where(row < ctx, s, -jnp.inf)
            sb[part, :] = s
            top = jnp.maximum(top, jnp.max(s.reshape(KC // 8, 8, block), axis=0))
        top = jnp.max(top, axis=0, keepdims=True)
        total = jnp.zeros((8, block), F32)
        delta = jnp.zeros((8, block), F32)
        for j in range(parts):
            part = slice(j * KC, (j + 1) * KC)
            e = jnp.exp2((sb[part, :] - top) * (SCALE * LOG2E))
            dp = dot(vb[part, :], g, NT)
            total = total + jnp.sum(e.reshape(KC // 8, 8, block), axis=0)
            delta = delta + jnp.sum((e * dp).reshape(KC // 8, 8, block), axis=0)
            eb[part, :] = e
            db[part, :] = dp
        inv = 1.0 / jnp.sum(total, axis=0, keepdims=True)
        delta = jnp.sum(delta, axis=0, keepdims=True) * inv
        inv_col = jnp.transpose(jnp.broadcast_to(inv, (HD, block)))
        gs = (g.astype(F32) * inv_col).astype(BF)
        qs = (q.astype(F32) * (inv_col * SCALE)).astype(BF)
        dqt = jnp.zeros((HD, block), F32)
        for j in range(parts):
            part = slice(j * KC, (j + 1) * KC)
            e = eb[part, :]
            ds = (e * (db[part, :] - delta)).astype(BF)
            dva[part, :] += dot(e.astype(BF), gs)
            dka[part, :] += dot(ds, qs)
            dqt = dqt + dot(kt[:, part], ds)
        dqs[here, :] = jnp.transpose(dqt * (inv * SCALE)).astype(BF)

        start_out(0, dqs, gq_out, t)

    def gh_copy(i):
        to = (sec + i) % secs
        return pltpu.make_async_remote_copy(
            hgs.at[rows(to, 2 * hown)],
            hgr.at[rows(i, 2 * hown)],
            gh_send.at[i],
            gh_recv.at[i],
            device_id=(to, grp),
            device_id_type=MESH,
        )

    gh_local = pltpu.make_async_copy(
        hgs.at[rows(sec, 2 * hown)], hgr.at[rows(0, 2 * hown)], gh_recv.at[0]
    )

    for i in range(secs):
        mine = slice(seq + i * hown, seq + (i + 1) * hown)
        hgs[2 * i * hown : (2 * i + 1) * hown, :] = dka[mine, :].astype(BF)
        hgs[(2 * i + 1) * hown : (2 * i + 2) * hown, :] = dva[mine, :].astype(BF)
    gh_local.start()

    @pl.loop(1, secs)
    def _(i):
        gh_copy(i).start()

    back = ((1, dks, gk_out), (2, dvs, gv_out))

    @pl.loop(0, chips)
    def _(i):
        t = chips - 1 - i
        here = rows(from_chip(t), block)
        dks[here, :] = dka[here, :].astype(BF)
        dvs[here, :] = dva[here, :].astype(BF)
        for a, src, dst in back:
            start_out(a, src, dst, t)

    gh_local.wait()

    @pl.loop(1, secs)
    def _(i):
        gh_copy(i).wait()

    acc = hgr[0 : 2 * hown, :].astype(F32)
    for i in range(1, secs):
        acc = acc + hgr[2 * i * hown : 2 * (i + 1) * hown, :].astype(F32)
    ghs[pl.ds(0, hown, stride=2), :] = acc[:hown, :]
    ghs[pl.ds(1, hown, stride=2), :] = acc[hown:, :]
    gh_copy_out.start()

    gh_copy_out.wait()

    @pl.loop(1, secs)
    def _(i):
        h_copy(i).wait_send()

    for a, src, dst in arrays:
        in_copy(a, src, dst, 0, 1).wait_send()
    out_copy(0, dqs, gq_out, 0, 1).wait()
    out_local(0, dqs, gq_out).wait()

    @pl.loop(1, chips)
    def _(i):
        t = turn(i)
        for dc in range(2):
            for a, src, dst in arrays:
                in_copy(a, src, dst, t, dc).wait_send()
            out_copy(0, dqs, gq_out, t, dc).wait()

    @pl.loop(1, chips)
    def _(i):
        for a, src, dst in back:
            for dc in range(2):
                out_copy(a, src, dst, chips - i, dc).wait()

    for a, src, dst in back:
        out_copy(a, src, dst, 0, 1).wait()
        out_local(a, src, dst).wait()


def settle_kernel(n, *refs):
    ins, outs, sem = refs[:n], refs[n : 2 * n], refs[2 * n]
    copies = [pltpu.make_async_copy(ins[i], outs[i], sem.at[i]) for i in range(n)]
    for copy in copies:
        copy.start()
    for copy in copies:
        copy.wait()


def settle(*arrays):
    n = len(arrays)
    anywhere = pl.BlockSpec(memory_space=pl.ANY)
    return pl.pallas_call(
        functools.partial(settle_kernel, n),
        out_shape=[jax.ShapeDtypeStruct(a.shape, a.dtype) for a in arrays],
        in_specs=[anywhere] * n,
        out_specs=[anywhere] * n,
        scratch_shapes=[pltpu.SemaphoreType.DMA((n,))],
        compiler_params=pltpu.CompilerParams(vmem_limit_bytes=8 * 2**20),
    )(*[pltpu.with_memory_space_constraint(a, pltpu.VMEM) for a in arrays])


def on_device(secs, grps, queries, keys, values, dout, history, context):
    own = queries.shape[0]
    hown = history.shape[0]
    seq = own * grps
    total = seq + hown * secs
    block = 2 * own
    hist = history.reshape(2 * hown, HD)
    anywhere = pl.BlockSpec(memory_space=pl.ANY)
    dma = pltpu.SemaphoreType.DMA
    args = (queries, keys, values, dout, hist, context)
    gq, gk, gv, gh = pl.pallas_call(
        functools.partial(kernel, secs, grps),
        out_shape=[
            pltpu.VMEM(queries.shape, BF),
            pltpu.VMEM(keys.shape, BF),
            pltpu.VMEM(values.shape, BF),
            pltpu.VMEM((2 * hown, HD), F32),
        ],
        in_specs=[anywhere] * 6,
        out_specs=[pl.BlockSpec(memory_space=pltpu.VMEM)] * 4,
        scratch_shapes=[
            pltpu.VMEM((seq, HD), BF),
            pltpu.VMEM((seq, HD), BF),
            pltpu.VMEM((total, HD), BF),
            pltpu.VMEM((total, HD), BF),
            pltpu.VMEM((HD, total), BF),
            pltpu.VMEM((total, block), F32),
            pltpu.VMEM((total, block), F32),
            pltpu.VMEM((total, block), F32),
            pltpu.VMEM((total, HD), F32),
            pltpu.VMEM((total, HD), F32),
            pltpu.VMEM((seq, HD), BF),
            pltpu.VMEM((seq, HD), BF),
            pltpu.VMEM((seq, HD), BF),
            pltpu.VMEM((2 * secs * hown, HD), BF),
            pltpu.VMEM((2 * secs * hown, HD), F32),
            pltpu.VMEM((2 * secs * hown, HD), BF),
            pltpu.VMEM((2 * secs * hown, HD), BF),
            dma((4, grps)),
            dma((4, grps)),
            dma((secs,)),
            dma((secs,)),
            dma((3, grps)),
            dma((3, grps)),
            dma((secs,)),
            dma((secs,)),
            pltpu.SemaphoreType.REGULAR,
            pltpu.SemaphoreType.REGULAR,
            pltpu.SemaphoreType.REGULAR((grps // 4 - 1,)),
            pltpu.SMEM((secs,), jnp.int32),
            pltpu.VMEM((2 * hown, HD), F32),
            dma((2,)),
        ],
        compiler_params=pltpu.CompilerParams(
            collective_id=0, has_side_effects=True, vmem_limit_bytes=VLIM * 2**20
        ),
    )(*[pltpu.with_memory_space_constraint(a, pltpu.HBM) for a in args])
    gq, gk, gv, gh = settle(gq, gk, gv, gh)
    return gq, gk, gv, gh.reshape(hown, 2, HD)


def solution(mesh):
    secs, grps = mesh.shape["sec"], mesh.shape["grp"]
    split = P(("sec", "grp"), None)
    return jax.shard_map(
        functools.partial(on_device, secs, grps),
        mesh=mesh,
        in_specs=(split, split, split, split, P("sec", None, "grp"), P()),
        out_specs=(split, split, split, P("sec", None, "grp")),
        check_vma=False,
    )
```

```python
import functools
import math

import jax
import jax.numpy as jnp
from jax import lax
from jax.experimental import pallas as pl
from jax.experimental.pallas import tpu as pltpu
from jax.sharding import PartitionSpec as P

HD = 128
MESH = pl.DeviceIdType.MESH
NT = (((1,), (1,)), ((), ()))
NN = (((1,), (0,)), ((), ()))
F32 = jnp.float32
BF = jnp.bfloat16
SCALE = HD ** (-0.5)
LOG2E = math.log2(math.e)
KC = 256
VLIM = 48


def dot(a, b, dims=NN):
    return lax.dot_general(a, b, dims, preferred_element_type=F32)


def kernel(
    secs,
    grps,
    q_in,
    k_in,
    v_in,
    g_in,
    h_in,
    ctx_in,
    gq_out,
    gk_out,
    gv_out,
    gh_out,
    qb,
    gb,
    kb,
    vb,
    kt,
    sb,
    eb,
    db,
    dka,
    dva,
    dqs,
    dks,
    dvs,
    hb,
    hf,
    hgs,
    hgr,
    in_send,
    in_recv,
    h_send,
    h_recv,
    out_send,
    out_recv,
    gh_send,
    gh_recv,
    line_sem,
    go_sem,
    ctx_all,
    ghs,
    own_sem,
):
    own = q_in.shape[0]
    chips = grps // 2
    block = 2 * own
    seq = grps * own
    hown = h_in.shape[0] // 2
    keys = seq + secs * hown
    parts = keys // KC
    sec = lax.axis_index("sec")
    grp = lax.axis_index("grp")
    z, core = grp // 2, grp % 2

    def shift(t):
        return ((t + 1) // 2) * (2 * (t % 2) - 1) + chips

    def turn(i):
        return i + ((i + 13) // 16) * (10 - 2 * i)

    def to_chip(t):
        return (z + shift(t)) % chips

    def from_chip(t):
        return (z - shift(t) + 2 * chips) % chips

    def device(chip, dc):
        return 2 * chip + (core + dc) % 2

    def cols(d):
        return pl.ds(pl.multiple_of(d * HD, HD), HD)

    def rows(d, n, base=0):
        return pl.ds(pl.multiple_of(base + d * n, n), n)

    def in_copy(a, src, dst, t, dc):
        to = device(to_chip(t), dc)
        return pltpu.make_async_remote_copy(
            src.at[:, cols(to)],
            dst.at[rows(grp, own)],
            in_send.at[a, 2 * t + dc],
            in_recv.at[a, 2 * t + dc],
            device_id=(sec, to),
            device_id_type=MESH,
        )

    def in_local(a, src, dst):
        return pltpu.make_async_copy(
            src.at[:, cols(grp)], dst.at[rows(grp, own)], in_recv.at[a, 0]
        )

    arrays = ((0, k_in, kb), (1, v_in, vb), (2, q_in, qb), (3, g_in, gb))

    def h_copy(i):
        return pltpu.make_async_remote_copy(
            h_in,
            hb.at[rows(sec, 2 * hown)],
            h_send.at[i],
            h_recv.at[i],
            device_id=((sec + i) % secs, grp),
            device_id_type=MESH,
        )

    h_local = pltpu.make_async_copy(h_in, hb.at[rows(sec, 2 * hown)], h_recv.at[0])

    beside = 2 * (chips // 2 + 1)
    leader = beside + 1
    barrier = pltpu.get_barrier_semaphore()
    for t in reversed(range(chips)):
        for dc in range(2):
            if t or dc:
                to = device(to_chip(t), dc)

                @pl.when(to != leader)
                def _(to=to):
                    pl.semaphore_signal(
                        barrier, 1, device_id=(sec, to), device_id_type=MESH
                    )

    for a, src, dst in arrays:
        in_local(a, src, dst).start()
    h_local.start()
    ctx_copy = pltpu.make_async_copy(ctx_in, ctx_all, own_sem.at[0])
    ctx_copy.start()
    gh_copy_out = pltpu.make_async_copy(ghs, gh_out, own_sem.at[1])

    @pl.when(grp != leader)
    def _():
        pl.semaphore_wait(barrier, grps - 1)

    @pl.when(grp == beside)
    def _():
        pl.semaphore_signal(line_sem, 1, device_id=(sec, leader), device_id_type=MESH)

    @pl.when(grp == leader)
    def _():
        pl.semaphore_wait(line_sem, 1)

        @pl.loop(1, secs)
        def _(i):
            pl.semaphore_signal(
                barrier, 1, device_id=((sec + i) % secs, grp), device_id_type=MESH
            )

    def all_there():
        @pl.when(grp == leader)
        def _():
            pl.semaphore_wait(barrier, secs - 1)

            @pl.loop(1, grps)
            def _(i):
                pl.semaphore_signal(
                    go_sem, 1, device_id=(sec, (grp + i) % grps), device_id_type=MESH
                )

        @pl.when(grp != leader)
        def _():
            pl.semaphore_wait(go_sem, 1)

    def start_in(first, last):
        for a, src, dst in arrays[first:last]:
            in_copy(a, src, dst, 0, 1).start()

        @pl.loop(1, chips)
        def _(i):
            t = turn(i)
            for a, src, dst in arrays[first:last]:
                in_copy(a, src, dst, t, 0).start()
                in_copy(a, src, dst, t, 1).start()

    start_in(0, 1)
    all_there()

    @pl.loop(1, secs)
    def _(i):
        h_copy(i).start()

    start_in(1, 2)
    start_in(2, 4)

    dka[...] = jnp.zeros_like(dka)
    dva[...] = jnp.zeros_like(dva)

    def wait_in(a, src, dst, t, dc):
        if dc == 0:

            @pl.when(t == 0)
            def _():
                in_local(a, src, dst).wait()

            @pl.when(t > 0)
            def _():
                in_copy(a, src, dst, t, dc).wait_recv()
        else:
            in_copy(a, src, dst, t, dc).wait_recv()

    h_local.wait()
    ctx_copy.wait()
    ctx = ctx_all[sec]

    @pl.loop(1, secs)
    def _(i):
        h_copy(i).wait_recv()

    hist = secs * hown
    hf[...] = hb[...].astype(F32)
    kb[seq:, :] = hf[pl.ds(0, hist, stride=2), :].astype(BF)
    vb[seq:, :] = hf[pl.ds(1, hist, stride=2), :].astype(BF)

    for j in range(seq, keys, KC):
        kt[:, j : j + KC] = kb[j : j + KC, :].T

    @pl.loop(0, chips)
    def _(i):
        t = turn(i)
        for dc in range(2):
            wait_in(*arrays[0], t, dc)
        here = rows(from_chip(t), block)
        kt[:, here] = kb[here, :].T

    @pl.loop(0, chips)
    def _(i):
        for dc in range(2):
            wait_in(*arrays[1], turn(i), dc)


    def out_copy(a, src, dst, t, dc):
        to = device(from_chip(t), dc)
        return pltpu.make_async_remote_copy(
            src.at[rows(to, own)],
            dst.at[:, cols(grp)],
            out_send.at[a, 2 * t + dc],
            out_recv.at[a, 2 * t + dc],
            device_id=(sec, to),
            device_id_type=MESH,
        )

    def out_local(a, src, dst):
        return pltpu.make_async_copy(
            src.at[rows(grp, own)], dst.at[:, cols(grp)], out_recv.at[a, 0]
        )

    def start_out(a, src, dst, t):
        out_copy(a, src, dst, t, 1).start()

        @pl.when(t == 0)
        def _():
            out_local(a, src, dst).start()

        @pl.when(t > 0)
        def _():
            out_copy(a, src, dst, t, 0).start()

    @pl.loop(0, chips)
    def _(i):
        t = turn(i)
        for a, src, dst in arrays[2:]:
            for dc in range(2):
                wait_in(a, src, dst, t, dc)
        here = rows(from_chip(t), block)
        q = qb[here, :]
        g = gb[here, :]
        top = jnp.full((8, block), -jnp.inf, F32)
        for j in range(parts):
            part = slice(j * KC, (j + 1) * KC)
            s = dot(kb[part, :], q, NT)
            if (j + 1) * KC > seq:
                row = lax.broadcasted_iota(jnp.int32, (KC, block), 0) + (j * KC - seq)
                s = jnp.where(row < ctx, s, -jnp.inf)
            sb[part, :] = s
            top = jnp.maximum(top, jnp.max(s.reshape(KC // 8, 8, block), axis=0))
        top = jnp.max(top, axis=0, keepdims=True)
        total = jnp.zeros((8, block), F32)
        delta = jnp.zeros((8, block), F32)
        for j in range(parts):
            part = slice(j * KC, (j + 1) * KC)
            e = jnp.exp2((sb[part, :] - top) * (SCALE * LOG2E))
            dp = dot(vb[part, :], g, NT)
            total = total + jnp.sum(e.reshape(KC // 8, 8, block), axis=0)
            delta = delta + jnp.sum((e * dp).reshape(KC // 8, 8, block), axis=0)
            eb[part, :] = e
            db[part, :] = dp
        inv = 1.0 / jnp.sum(total, axis=0, keepdims=True)
        delta = jnp.sum(delta, axis=0, keepdims=True) * inv
        inv_col = jnp.transpose(jnp.broadcast_to(inv, (HD, block)))
        gs = (g.astype(F32) * inv_col).astype(BF)
        qs = (q.astype(F32) * (inv_col * SCALE)).astype(BF)
        dqt = jnp.zeros((HD, block), F32)
        for j in range(parts):
            part = slice(j * KC, (j + 1) * KC)
            e = eb[part, :]
            ds = (e * (db[part, :] - delta)).astype(BF)
            dva[part, :] += dot(e.astype(BF), gs)
            dka[part, :] += dot(ds, qs)
            dqt = dqt + dot(kt[:, part], ds)
        dqs[here, :] = jnp.transpose(dqt * (inv * SCALE)).astype(BF)

        start_out(0, dqs, gq_out, t)

    def gh_copy(i):
        to = (sec + i) % secs
        return pltpu.make_async_remote_copy(
            hgs.at[rows(to, 2 * hown)],
            hgr.at[rows(i, 2 * hown)],
            gh_send.at[i],
            gh_recv.at[i],
            device_id=(to, grp),
            device_id_type=MESH,
        )

    gh_local = pltpu.make_async_copy(
        hgs.at[rows(sec, 2 * hown)], hgr.at[rows(0, 2 * hown)], gh_recv.at[0]
    )

    back = ((1, dks, gk_out), (2, dvs, gv_out))

    def return_chip(t):
        here = rows(from_chip(t), block)
        dks[here, :] = dka[here, :].astype(BF)
        dvs[here, :] = dva[here, :].astype(BF)
        for a, src, dst in back:
            start_out(a, src, dst, t)

    return_chip(chips - 1)
    return_chip(chips - 2)

    for i in range(secs):
        mine = slice(seq + i * hown, seq + (i + 1) * hown)
        hgs[2 * i * hown : (2 * i + 1) * hown, :] = dka[mine, :].astype(BF)
        hgs[(2 * i + 1) * hown : (2 * i + 2) * hown, :] = dva[mine, :].astype(BF)
    gh_local.start()

    @pl.loop(1, secs)
    def _(i):
        gh_copy(i).start()

    @pl.loop(2, chips)
    def _(i):
        return_chip(chips - 1 - i)

    gh_local.wait()

    @pl.loop(1, secs)
    def _(i):
        gh_copy(i).wait()

    acc = hgr[0 : 2 * hown, :].astype(F32)
    for i in range(1, secs):
        acc = acc + hgr[2 * i * hown : 2 * (i + 1) * hown, :].astype(F32)
    ghs[pl.ds(0, hown, stride=2), :] = acc[:hown, :]
    ghs[pl.ds(1, hown, stride=2), :] = acc[hown:, :]
    gh_copy_out.start()

    gh_copy_out.wait()

    @pl.loop(1, secs)
    def _(i):
        h_copy(i).wait_send()

    for a, src, dst in arrays:
        in_copy(a, src, dst, 0, 1).wait_send()
    out_copy(0, dqs, gq_out, 0, 1).wait()
    out_local(0, dqs, gq_out).wait()

    @pl.loop(1, chips)
    def _(i):
        t = turn(i)
        for dc in range(2):
            for a, src, dst in arrays:
                in_copy(a, src, dst, t, dc).wait_send()
            out_copy(0, dqs, gq_out, t, dc).wait()

    @pl.loop(1, chips)
    def _(i):
        for a, src, dst in back:
            for dc in range(2):
                out_copy(a, src, dst, chips - i, dc).wait()

    for a, src, dst in back:
        out_copy(a, src, dst, 0, 1).wait()
        out_local(a, src, dst).wait()


def settle_kernel(n, *refs):
    ins, outs, sem = refs[:n], refs[n : 2 * n], refs[2 * n]
    copies = [pltpu.make_async_copy(ins[i], outs[i], sem.at[i]) for i in range(n)]
    for copy in copies:
        copy.start()
    for copy in copies:
        copy.wait()


def settle(*arrays):
    n = len(arrays)
    anywhere = pl.BlockSpec(memory_space=pl.ANY)
    return pl.pallas_call(
        functools.partial(settle_kernel, n),
        out_shape=[jax.ShapeDtypeStruct(a.shape, a.dtype) for a in arrays],
        in_specs=[anywhere] * n,
        out_specs=[anywhere] * n,
        scratch_shapes=[pltpu.SemaphoreType.DMA((n,))],
        compiler_params=pltpu.CompilerParams(vmem_limit_bytes=8 * 2**20),
    )(*[pltpu.with_memory_space_constraint(a, pltpu.VMEM) for a in arrays])


def on_device(secs, grps, queries, keys, values, dout, history, context):
    own = queries.shape[0]
    hown = history.shape[0]
    seq = own * grps
    total = seq + hown * secs
    block = 2 * own
    hist = history.reshape(2 * hown, HD)
    anywhere = pl.BlockSpec(memory_space=pl.ANY)
    dma = pltpu.SemaphoreType.DMA
    args = (queries, keys, values, dout, hist, context)
    gq, gk, gv, gh = pl.pallas_call(
        functools.partial(kernel, secs, grps),
        out_shape=[
            pltpu.VMEM(queries.shape, BF),
            pltpu.VMEM(keys.shape, BF),
            pltpu.VMEM(values.shape, BF),
            pltpu.VMEM((2 * hown, HD), F32),
        ],
        in_specs=[anywhere] * 6,
        out_specs=[pl.BlockSpec(memory_space=pltpu.VMEM)] * 4,
        scratch_shapes=[
            pltpu.VMEM((seq, HD), BF),
            pltpu.VMEM((seq, HD), BF),
            pltpu.VMEM((total, HD), BF),
            pltpu.VMEM((total, HD), BF),
            pltpu.VMEM((HD, total), BF),
            pltpu.VMEM((total, block), F32),
            pltpu.VMEM((total, block), F32),
            pltpu.VMEM((total, block), F32),
            pltpu.VMEM((total, HD), F32),
            pltpu.VMEM((total, HD), F32),
            pltpu.VMEM((seq, HD), BF),
            pltpu.VMEM((seq, HD), BF),
            pltpu.VMEM((seq, HD), BF),
            pltpu.VMEM((2 * secs * hown, HD), BF),
            pltpu.VMEM((2 * secs * hown, HD), F32),
            pltpu.VMEM((2 * secs * hown, HD), BF),
            pltpu.VMEM((2 * secs * hown, HD), BF),
            dma((4, grps)),
            dma((4, grps)),
            dma((secs,)),
            dma((secs,)),
            dma((3, grps)),
            dma((3, grps)),
            dma((secs,)),
            dma((secs,)),
            pltpu.SemaphoreType.REGULAR,
            pltpu.SemaphoreType.REGULAR,
            pltpu.SMEM((secs,), jnp.int32),
            pltpu.VMEM((2 * hown, HD), F32),
            dma((2,)),
        ],
        compiler_params=pltpu.CompilerParams(
            collective_id=0, has_side_effects=True, vmem_limit_bytes=VLIM * 2**20
        ),
    )(*[pltpu.with_memory_space_constraint(a, pltpu.HBM) for a in args])
    gq, gk, gv, gh = settle(gq, gk, gv, gh)
    return gq, gk, gv, gh.reshape(hown, 2, HD)


def solution(mesh):
    secs, grps = mesh.shape["sec"], mesh.shape["grp"]
    split = P(("sec", "grp"), None)
    return jax.shard_map(
        functools.partial(on_device, secs, grps),
        mesh=mesh,
        in_specs=(split, split, split, split, P("sec", None, "grp"), P()),
        out_specs=(split, split, split, P("sec", None, "grp")),
        check_vma=False,
    )
```

```python
import functools
import math

import jax
import jax.numpy as jnp
from jax import lax
from jax.experimental import pallas as pl
from jax.experimental.pallas import tpu as pltpu
from jax.sharding import PartitionSpec as P

HD = 128
MESH = pl.DeviceIdType.MESH
NT = (((1,), (1,)), ((), ()))
NN = (((1,), (0,)), ((), ()))
F32 = jnp.float32
BF = jnp.bfloat16
SCALE = HD ** (-0.5)
LOG2E = math.log2(math.e)
KC = 256
VLIM = 48


def dot(a, b, dims=NN):
    return lax.dot_general(a, b, dims, preferred_element_type=F32)


def kernel(
    secs,
    grps,
    q_in,
    k_in,
    v_in,
    g_in,
    h_in,
    ctx_in,
    gq_out,
    gk_out,
    gv_out,
    gh_out,
    qb,
    gb,
    kb,
    vb,
    kt,
    sb,
    eb,
    db,
    dka,
    dva,
    dqs,
    dks,
    dvs,
    hb,
    hf,
    hgs,
    hgr,
    in_send,
    in_recv,
    h_send,
    h_recv,
    out_send,
    out_recv,
    gh_send,
    gh_recv,
    line_sem,
    go_sem,
    ctx_all,
    ghs,
    own_sem,
):
    own = q_in.shape[0]
    chips = grps // 2
    block = 2 * own
    seq = grps * own
    hown = h_in.shape[0] // 2
    keys = seq + secs * hown
    parts = keys // KC
    sec = lax.axis_index("sec")
    grp = lax.axis_index("grp")
    z, core = grp // 2, grp % 2

    def shift(t):
        return ((t + 1) // 2) * (2 * (t % 2) - 1) + chips

    def turn(i):
        return i + ((i + 13) // 16) * (10 - 2 * i)

    def to_chip(t):
        return (z + shift(t)) % chips

    def from_chip(t):
        return (z - shift(t) + 2 * chips) % chips

    def device(chip, dc):
        return 2 * chip + (core + dc) % 2

    def cols(d):
        return pl.ds(pl.multiple_of(d * HD, HD), HD)

    def rows(d, n, base=0):
        return pl.ds(pl.multiple_of(base + d * n, n), n)

    def in_copy(a, src, dst, t, dc):
        to = device(to_chip(t), dc)
        return pltpu.make_async_remote_copy(
            src.at[:, cols(to)],
            dst.at[rows(grp, own)],
            in_send.at[a, 2 * t + dc],
            in_recv.at[a, 2 * t + dc],
            device_id=(sec, to),
            device_id_type=MESH,
        )

    def in_local(a, src, dst):
        return pltpu.make_async_copy(
            src.at[:, cols(grp)], dst.at[rows(grp, own)], in_recv.at[a, 0]
        )

    arrays = ((0, k_in, kb), (1, v_in, vb), (2, q_in, qb), (3, g_in, gb))

    def h_copy(i):
        return pltpu.make_async_remote_copy(
            h_in,
            hb.at[rows(sec, 2 * hown)],
            h_send.at[i],
            h_recv.at[i],
            device_id=((sec + i) % secs, grp),
            device_id_type=MESH,
        )

    h_local = pltpu.make_async_copy(h_in, hb.at[rows(sec, 2 * hown)], h_recv.at[0])

    beside = 2 * (chips // 2 + 1)
    leader = beside + 1
    barrier = pltpu.get_barrier_semaphore()
    for t in reversed(range(chips)):
        for dc in range(2):
            if t or dc:
                to = device(to_chip(t), dc)

                @pl.when(to != leader)
                def _(to=to):
                    pl.semaphore_signal(
                        barrier, 1, device_id=(sec, to), device_id_type=MESH
                    )

    for a, src, dst in arrays:
        in_local(a, src, dst).start()
    h_local.start()
    ctx_copy = pltpu.make_async_copy(ctx_in, ctx_all, own_sem.at[0])
    ctx_copy.start()
    gh_copy_out = pltpu.make_async_copy(ghs, gh_out, own_sem.at[1])

    @pl.when(grp != leader)
    def _():
        pl.semaphore_wait(barrier, grps - 1)

    @pl.when(grp == beside)
    def _():
        pl.semaphore_signal(line_sem, 1, device_id=(sec, leader), device_id_type=MESH)

    @pl.when(grp == leader)
    def _():
        pl.semaphore_wait(line_sem, 1)

        @pl.loop(1, secs)
        def _(i):
            pl.semaphore_signal(
                barrier, 1, device_id=((sec + i) % secs, grp), device_id_type=MESH
            )

    def all_there():
        @pl.when(grp == leader)
        def _():
            pl.semaphore_wait(barrier, secs - 1)

            @pl.loop(1, grps)
            def _(i):
                pl.semaphore_signal(
                    go_sem, 1, device_id=(sec, (grp + i) % grps), device_id_type=MESH
                )

        @pl.when(grp != leader)
        def _():
            pl.semaphore_wait(go_sem, 1)

    def start_in(first, last):
        for a, src, dst in arrays[first:last]:
            in_copy(a, src, dst, 0, 1).start()

        @pl.loop(1, chips)
        def _(i):
            t = turn(i)
            for a, src, dst in arrays[first:last]:
                in_copy(a, src, dst, t, 0).start()
                in_copy(a, src, dst, t, 1).start()

    start_in(0, 2)
    all_there()

    @pl.loop(1, secs)
    def _(i):
        h_copy(i).start()

    start_in(2, 4)

    dka[...] = jnp.zeros_like(dka)
    dva[...] = jnp.zeros_like(dva)

    def wait_in(a, src, dst, t, dc):
        if dc == 0:

            @pl.when(t == 0)
            def _():
                in_local(a, src, dst).wait()

            @pl.when(t > 0)
            def _():
                in_copy(a, src, dst, t, dc).wait_recv()
        else:
            in_copy(a, src, dst, t, dc).wait_recv()

    h_local.wait()
    ctx_copy.wait()
    ctx = ctx_all[sec]

    @pl.loop(1, secs)
    def _(i):
        h_copy(i).wait_recv()

    hist = secs * hown
    hf[...] = hb[...].astype(F32)
    kb[seq:, :] = hf[pl.ds(0, hist, stride=2), :].astype(BF)
    vb[seq:, :] = hf[pl.ds(1, hist, stride=2), :].astype(BF)

    for j in range(seq, keys, KC):
        kt[:, j : j + KC] = kb[j : j + KC, :].T

    @pl.loop(0, chips)
    def _(i):
        t = turn(i)
        for dc in range(2):
            wait_in(*arrays[0], t, dc)
        here = rows(from_chip(t), block)
        kt[:, here] = kb[here, :].T

    @pl.loop(0, chips)
    def _(i):
        for dc in range(2):
            wait_in(*arrays[1], turn(i), dc)


    def out_copy(a, src, dst, t, dc):
        to = device(from_chip(t), dc)
        return pltpu.make_async_remote_copy(
            src.at[rows(to, own)],
            dst.at[:, cols(grp)],
            out_send.at[a, 2 * t + dc],
            out_recv.at[a, 2 * t + dc],
            device_id=(sec, to),
            device_id_type=MESH,
        )

    def out_local(a, src, dst):
        return pltpu.make_async_copy(
            src.at[rows(grp, own)], dst.at[:, cols(grp)], out_recv.at[a, 0]
        )

    def start_out(a, src, dst, t):
        out_copy(a, src, dst, t, 1).start()

        @pl.when(t == 0)
        def _():
            out_local(a, src, dst).start()

        @pl.when(t > 0)
        def _():
            out_copy(a, src, dst, t, 0).start()

    @pl.loop(0, chips)
    def _(i):
        t = turn(i)
        for a, src, dst in arrays[2:]:
            for dc in range(2):
                wait_in(a, src, dst, t, dc)
        here = rows(from_chip(t), block)
        q = qb[here, :]
        g = gb[here, :]
        top = jnp.full((8, block), -jnp.inf, F32)
        for j in range(parts):
            part = slice(j * KC, (j + 1) * KC)
            s = dot(kb[part, :], q, NT)
            if (j + 1) * KC > seq:
                row = lax.broadcasted_iota(jnp.int32, (KC, block), 0) + (j * KC - seq)
                s = jnp.where(row < ctx, s, -jnp.inf)
            sb[part, :] = s
            top = jnp.maximum(top, jnp.max(s.reshape(KC // 8, 8, block), axis=0))
        top = jnp.max(top, axis=0, keepdims=True)
        total = jnp.zeros((8, block), F32)
        delta = jnp.zeros((8, block), F32)
        for j in range(parts):
            part = slice(j * KC, (j + 1) * KC)
            e = jnp.exp2((sb[part, :] - top) * (SCALE * LOG2E))
            dp = dot(vb[part, :], g, NT)
            total = total + jnp.sum(e.reshape(KC // 8, 8, block), axis=0)
            delta = delta + jnp.sum((e * dp).reshape(KC // 8, 8, block), axis=0)
            eb[part, :] = e
            db[part, :] = dp
        inv = 1.0 / jnp.sum(total, axis=0, keepdims=True)
        delta = jnp.sum(delta, axis=0, keepdims=True) * inv
        inv_col = jnp.transpose(jnp.broadcast_to(inv, (HD, block)))
        gs = (g.astype(F32) * inv_col).astype(BF)
        qs = (q.astype(F32) * (inv_col * SCALE)).astype(BF)
        dqt = jnp.zeros((HD, block), F32)
        for j in range(parts):
            part = slice(j * KC, (j + 1) * KC)
            e = eb[part, :]
            ds = (e * (db[part, :] - delta)).astype(BF)
            dva[part, :] += dot(e.astype(BF), gs)
            dka[part, :] += dot(ds, qs)
            dqt = dqt + dot(kt[:, part], ds)
        dqs[here, :] = jnp.transpose(dqt * (inv * SCALE)).astype(BF)

        start_out(0, dqs, gq_out, t)

    def gh_copy(i):
        to = (sec + i) % secs
        return pltpu.make_async_remote_copy(
            hgs.at[rows(to, 2 * hown)],
            hgr.at[rows(i, 2 * hown)],
            gh_send.at[i],
            gh_recv.at[i],
            device_id=(to, grp),
            device_id_type=MESH,
        )

    gh_local = pltpu.make_async_copy(
        hgs.at[rows(sec, 2 * hown)], hgr.at[rows(0, 2 * hown)], gh_recv.at[0]
    )

    back = ((1, dks, gk_out), (2, dvs, gv_out))

    def return_chip(t):
        here = rows(from_chip(t), block)
        dks[here, :] = dka[here, :].astype(BF)
        dvs[here, :] = dva[here, :].astype(BF)
        for a, src, dst in back:
            start_out(a, src, dst, t)

    return_chip(chips - 1)
    return_chip(chips - 2)

    for i in range(secs):
        mine = slice(seq + i * hown, seq + (i + 1) * hown)
        hgs[2 * i * hown : (2 * i + 1) * hown, :] = dka[mine, :].astype(BF)
        hgs[(2 * i + 1) * hown : (2 * i + 2) * hown, :] = dva[mine, :].astype(BF)
    gh_local.start()

    @pl.loop(1, secs)
    def _(i):
        gh_copy(i).start()

    @pl.loop(2, chips)
    def _(i):
        return_chip(chips - 1 - i)

    gh_local.wait()

    @pl.loop(1, secs)
    def _(i):
        gh_copy(i).wait()

    acc = hgr[0 : 2 * hown, :].astype(F32)
    for i in range(1, secs):
        acc = acc + hgr[2 * i * hown : 2 * (i + 1) * hown, :].astype(F32)
    ghs[pl.ds(0, hown, stride=2), :] = acc[:hown, :]
    ghs[pl.ds(1, hown, stride=2), :] = acc[hown:, :]
    gh_copy_out.start()

    gh_copy_out.wait()

    @pl.loop(1, secs)
    def _(i):
        h_copy(i).wait_send()

    for a, src, dst in arrays:
        in_copy(a, src, dst, 0, 1).wait_send()
    out_copy(0, dqs, gq_out, 0, 1).wait()
    out_local(0, dqs, gq_out).wait()

    @pl.loop(1, chips)
    def _(i):
        t = turn(i)
        for dc in range(2):
            for a, src, dst in arrays:
                in_copy(a, src, dst, t, dc).wait_send()
            out_copy(0, dqs, gq_out, t, dc).wait()

    @pl.loop(1, chips)
    def _(i):
        for a, src, dst in back:
            for dc in range(2):
                out_copy(a, src, dst, chips - i, dc).wait()

    for a, src, dst in back:
        out_copy(a, src, dst, 0, 1).wait()
        out_local(a, src, dst).wait()


def settle_kernel(n, *refs):
    ins, outs, sem = refs[:n], refs[n : 2 * n], refs[2 * n]
    copies = [pltpu.make_async_copy(ins[i], outs[i], sem.at[i]) for i in range(n)]
    for copy in copies:
        copy.start()
    for copy in copies:
        copy.wait()


def settle(*arrays):
    n = len(arrays)
    anywhere = pl.BlockSpec(memory_space=pl.ANY)
    return pl.pallas_call(
        functools.partial(settle_kernel, n),
        out_shape=[jax.ShapeDtypeStruct(a.shape, a.dtype) for a in arrays],
        in_specs=[anywhere] * n,
        out_specs=[anywhere] * n,
        scratch_shapes=[pltpu.SemaphoreType.DMA((n,))],
        compiler_params=pltpu.CompilerParams(vmem_limit_bytes=8 * 2**20),
    )(*[pltpu.with_memory_space_constraint(a, pltpu.VMEM) for a in arrays])


def on_device(secs, grps, queries, keys, values, dout, history, context):
    own = queries.shape[0]
    hown = history.shape[0]
    seq = own * grps
    total = seq + hown * secs
    block = 2 * own
    hist = history.reshape(2 * hown, HD)
    anywhere = pl.BlockSpec(memory_space=pl.ANY)
    dma = pltpu.SemaphoreType.DMA
    args = (queries, keys, values, dout, hist, context)
    gq, gk, gv, gh = pl.pallas_call(
        functools.partial(kernel, secs, grps),
        out_shape=[
            pltpu.VMEM(queries.shape, BF),
            pltpu.VMEM(keys.shape, BF),
            pltpu.VMEM(values.shape, BF),
            pltpu.VMEM((2 * hown, HD), F32),
        ],
        in_specs=[anywhere] * 6,
        out_specs=[pl.BlockSpec(memory_space=pltpu.VMEM)] * 4,
        scratch_shapes=[
            pltpu.VMEM((seq, HD), BF),
            pltpu.VMEM((seq, HD), BF),
            pltpu.VMEM((total, HD), BF),
            pltpu.VMEM((total, HD), BF),
            pltpu.VMEM((HD, total), BF),
            pltpu.VMEM((total, block), F32),
            pltpu.VMEM((total, block), F32),
            pltpu.VMEM((total, block), F32),
            pltpu.VMEM((total, HD), F32),
            pltpu.VMEM((total, HD), F32),
            pltpu.VMEM((seq, HD), BF),
            pltpu.VMEM((seq, HD), BF),
            pltpu.VMEM((seq, HD), BF),
            pltpu.VMEM((2 * secs * hown, HD), BF),
            pltpu.VMEM((2 * secs * hown, HD), F32),
            pltpu.VMEM((2 * secs * hown, HD), BF),
            pltpu.VMEM((2 * secs * hown, HD), BF),
            dma((4, grps)),
            dma((4, grps)),
            dma((secs,)),
            dma((secs,)),
            dma((3, grps)),
            dma((3, grps)),
            dma((secs,)),
            dma((secs,)),
            pltpu.SemaphoreType.REGULAR,
            pltpu.SemaphoreType.REGULAR,
            pltpu.SMEM((secs,), jnp.int32),
            pltpu.VMEM((2 * hown, HD), F32),
            dma((2,)),
        ],
        compiler_params=pltpu.CompilerParams(
            collective_id=0, has_side_effects=True, vmem_limit_bytes=VLIM * 2**20
        ),
    )(*[pltpu.with_memory_space_constraint(a, pltpu.HBM) for a in args])
    gq, gk, gv, gh = settle(gq, gk, gv, gh)
    return gq, gk, gv, gh.reshape(hown, 2, HD)


def solution(mesh):
    secs, grps = mesh.shape["sec"], mesh.shape["grp"]
    split = P(("sec", "grp"), None)
    return jax.shard_map(
        functools.partial(on_device, secs, grps),
        mesh=mesh,
        in_specs=(split, split, split, split, P("sec", None, "grp"), P()),
        out_specs=(split, split, split, P("sec", None, "grp")),
        check_vma=False,
    )
```
